32 devices in a mesh: groups: 2 (over y), seq: 8 (over z, x), head: 2 (over core).
Axes of the slice: x: 2, y: 2, z: 4, core: 2. Of those that a mesh axis runs over, the one named last changes fastest.
Arguments:
- queries: bfloat16 [2048, 768], P(('groups', 'seq'), 'head'), parts along dimension 0, may hold values from -6.5 to 6.5
- key_rows: bfloat16 [2048, 768], P(('groups', 'seq'), 'head'), parts along dimension 0, may hold values from -6.5 to 6.5
- value_rows: bfloat16 [2048, 768], P(('groups', 'seq'), 'head'), parts along dimension 0, may hold values from -6 to 6
- grad_out: bfloat16 [2048, 768], P(('groups', 'seq'), 'head'), parts along dimension 0, may hold values from -6 to 6
- offsets: int32 [8, 16], replicated, may hold values from 0 to 127, as said below
Outputs:
- attended: bfloat16 [2048, 768], P(('groups', 'seq'), 'head'), parts along dimension 0
- grad_query: bfloat16 [2048, 768], P(('groups', 'seq'), 'head'), parts along dimension 0
- grad_key: bfloat16 [2048, 768], P(('groups', 'seq'), 'head'), parts along dimension 0
- grad_value: bfloat16 [2048, 768], P(('groups', 'seq'), 'head'), parts along dimension 0
The draws below stay inside these ranges and needn't reach their ends.
There are 2 independent parts, one for each index of `groups`. The reference program is written for one: setup_inputs(seed, part) draws one part's arguments, and reference() takes and returns one part's arrays. A program takes and returns all parts, laid end to end along the dimension named above; an argument that names none is the same for every part. Nothing has to cross between parts.
Inputs may be any that keep to these rules, and one draw needn't show every extreme that they name: offsets[l, h] lies in 0 to 2^l - 1 at level l, and at every level some head takes 2^l - 1.
All inputs are finite; a program needn't handle non-finite values.
Results may differ from the reference program's by a relative error of at most 0.019.
Values may be sent and summed in bfloat16 or wider, within the bound.
A program may use at most 128 MiB of HBM per device.

```python
import jax
import jax.numpy as jnp
from jax import lax

HEADS = 16
HDIM = 48
LEVELS = 8
LENGTH = 1024


def draw_queries(key, part):
    key = jax.random.fold_in(key, 11)
    values = jnp.clip(1.6 * jax.random.normal(key, (LENGTH, HEADS, HDIM), jnp.float32), -6.5, 6.5)
    return values.reshape(LENGTH, HEADS * HDIM).astype(jnp.bfloat16)


def draw_key_rows(key, part):
    key = jax.random.fold_in(key, 12)
    values = jnp.clip(1.6 * jax.random.normal(key, (LENGTH, HEADS, HDIM), jnp.float32), -6.5, 6.5)
    return values.reshape(LENGTH, HEADS * HDIM).astype(jnp.bfloat16)


def draw_offsets(key, part):
    key = jax.random.fold_in(key, 13)
    first_key, second_key = jax.random.split(key)
    level_span = 2 ** jnp.arange(LEVELS, dtype=jnp.int32)
    drawn = jax.random.randint(first_key, (LEVELS, HEADS), 0, level_span[:, None])
    pinned = jax.random.randint(second_key, (LEVELS, 1), 0, HEADS)
    head_ids = jnp.arange(HEADS, dtype=jnp.int32)[None, :]
    return jnp.where(head_ids == pinned, level_span[:, None] - 1, drawn).astype(jnp.int32)


def block_scale(key, shape, shards, low, top_value):
    level, own = 1.0, jax.random.fold_in(key, 6)
    for dim, parts in shards:
        draws = jnp.exp(jax.random.uniform(jax.random.fold_in(own, dim), (parts,), jnp.float32, low / len(shards), top_value / len(shards)))
        level = level * jnp.repeat(draws, shape[dim] // parts).reshape([-1 if axis == dim else 1 for axis in range(len(shape))])
    return level


def scatter_about(key, extent, scale, most, cuts=(), held_as=jnp.bfloat16):
    gain = block_scale(key, extent, cuts, -0.22, 0.18) if cuts else 1.0
    values = jax.random.normal(key, extent, jnp.float32) * scale * gain
    return jnp.minimum(jnp.maximum(values, -most), most).astype(held_as)


def setup_inputs(seed: int = 0, part: int = 0) -> dict:
    splits = jax.random.split(jax.random.key(seed), 6)
    part_keys = jax.random.split(jax.random.fold_in(splits[5], part), 6)
    queries = draw_queries(jax.random.fold_in(jax.random.fold_in(splits[5], part), 71), part)
    key_rows = draw_key_rows(jax.random.fold_in(jax.random.fold_in(splits[5], part), 71), part)
    value_rows = scatter_about(part_keys[2], (LENGTH, HEADS * HDIM), 1.0, 6.0, ((0, 8), (1, 2)))
    grad_out = scatter_about(part_keys[3], (LENGTH, HEADS * HDIM), 1.0, 6.0, ((0, 8), (1, 2)))
    offsets = draw_offsets(jax.random.fold_in(splits[5], 71), part)
    return {"queries": queries, "key_rows": key_rows, "value_rows": value_rows, "grad_out": grad_out, "offsets": offsets}


def pick_rows(values, level_offsets, stride):
    length, head_count = values.shape[0], values.shape[1]
    trailing = values.shape[2:]
    grouped = values.reshape((length // stride, stride, head_count) + trailing)
    chosen_pos = level_offsets.astype(jnp.int32).reshape((1, 1, head_count) + (1,) * len(trailing))
    chosen_pos = jnp.broadcast_to(chosen_pos, (length // stride, 1, head_count) + trailing)
    return jnp.take_along_axis(grouped, chosen_pos, axis=1)[:, 0]


def spread_rows(values, level_offsets, stride, fill):
    count, head_count = values.shape[0], values.shape[1]
    trailing = values.shape[2:]
    marks = jnp.arange(stride, dtype=jnp.int32)[:, None] == level_offsets.astype(jnp.int32)[None, :]
    marks = marks.reshape((1, stride, head_count) + (1,) * len(trailing))
    placed = jnp.where(marks, values[:, None], jnp.asarray(fill, values.dtype))
    return placed.reshape((count * stride, head_count) + trailing)


def segments_by_head(values, segment):
    count, head_count = values.shape[0], values.shape[1]
    trailing = values.shape[2:]
    shaped = values.reshape((count // segment, segment, head_count) + trailing)
    return jnp.transpose(shaped, (2, 0, 1) + tuple(range(3, 3 + len(trailing))))


def heads_back(values):
    trailing = values.shape[3:]
    moved = jnp.transpose(values, (1, 2, 0) + tuple(range(3, 3 + len(trailing))))
    return moved.reshape((moved.shape[0] * moved.shape[1], moved.shape[2]) + trailing)


def head_forward(inputs):
    query_seg, key_seg, value_seg = inputs
    factor = query_seg.shape[-1] ** -0.5
    scores = jnp.einsum("nid,njd->nij", query_seg.astype(jnp.float32), key_seg.astype(jnp.float32)) * factor
    largest = jnp.max(scores, axis=2)
    powers = jnp.exp(scores - largest[..., None])
    totals = jnp.sum(powers, axis=2)
    rounded = lax.optimization_barrier(powers.astype(jnp.bfloat16)).astype(jnp.float32)
    summed = jnp.einsum("nij,njd->nid", rounded, value_seg.astype(jnp.float32))
    return largest, totals, summed


def head_backward(inputs):
    query_seg, key_seg, value_seg, outgrad_seg, total_seg, dot_seg = inputs
    factor = query_seg.shape[-1] ** -0.5
    query_wide = query_seg.astype(jnp.float32)
    key_wide = key_seg.astype(jnp.float32)
    value_wide = value_seg.astype(jnp.float32)
    outgrad_wide = outgrad_seg.astype(jnp.float32)
    scores = jnp.einsum("nid,njd->nij", query_wide, key_wide) * factor
    weights = jnp.exp(scores - total_seg[..., None])
    weights_low = lax.optimization_barrier(weights.astype(jnp.bfloat16)).astype(jnp.float32)
    value_grad = jnp.einsum("nij,nid->njd", weights_low, outgrad_wide)
    grad_prob = jnp.einsum("nid,njd->nij", outgrad_wide, value_wide)
    grad_score = weights * (grad_prob - dot_seg[..., None])
    grad_score = lax.optimization_barrier(grad_score.astype(jnp.bfloat16)).astype(jnp.float32)
    query_grad = jnp.einsum("nij,njd->nid", grad_score, key_wide) * factor
    key_grad = jnp.einsum("nij,nid->njd", grad_score, query_wide) * factor
    return query_grad, key_grad, value_grad


def reference(queries, key_rows, value_rows, grad_out, offsets):
    length, width = queries.shape
    head_count = offsets.shape[1]
    head_dim = width // head_count
    segment = length // 2 ** (LEVELS - 1)
    query_all = queries.reshape(length, head_count, head_dim)
    key_all = key_rows.reshape(length, head_count, head_dim)
    value_all = value_rows.reshape(length, head_count, head_dim)
    outgrad_all = grad_out.reshape(length, head_count, head_dim)
    for level_no in range(LEVELS):
        stride = 2 ** level_no
        level_offsets = offsets[level_no]
        level_parts = tuple(segments_by_head(pick_rows(source, level_offsets, stride), segment)
                            for source in (query_all, key_all, value_all))
        largest, totals, summed = lax.map(head_forward, level_parts)
        level_max = spread_rows(heads_back(largest), level_offsets, stride, -jnp.inf)
        level_total = spread_rows(heads_back(totals), level_offsets, stride, 0.0)
        level_sum = spread_rows(heads_back(summed), level_offsets, stride, 0.0)
        if level_no == 0:
            running_max, running_total, running_sum = level_max, level_total, level_sum
        else:
            newest_max = jnp.maximum(running_max, level_max)
            old_scale = jnp.exp(running_max - newest_max)
            new_scale = jnp.exp(level_max - newest_max)
            running_total = running_total * old_scale + level_total * new_scale
            running_sum = running_sum * old_scale[..., None] + level_sum * new_scale[..., None]
            running_max = newest_max
    attended = (running_sum / running_total[..., None]).astype(jnp.bfloat16)
    log_total = running_max + jnp.log(running_total)
    dot_rows = jnp.sum(outgrad_all.astype(jnp.float32) * attended.astype(jnp.float32), axis=2)
    grad_q_sum = jnp.zeros((length, head_count, head_dim), jnp.float32)
    grad_k_sum = jnp.zeros((length, head_count, head_dim), jnp.float32)
    grad_v_sum = jnp.zeros((length, head_count, head_dim), jnp.float32)
    for level_no in range(LEVELS):
        stride = 2 ** level_no
        level_offsets = offsets[level_no]
        level_parts = tuple(segments_by_head(pick_rows(source, level_offsets, stride), segment)
                            for source in (query_all, key_all, value_all, outgrad_all, log_total, dot_rows))
        query_grad, key_grad, value_grad = lax.map(head_backward, level_parts)
        grad_q_sum = grad_q_sum + spread_rows(heads_back(query_grad), level_offsets, stride, 0.0)
        grad_k_sum = grad_k_sum + spread_rows(heads_back(key_grad), level_offsets, stride, 0.0)
        grad_v_sum = grad_v_sum + spread_rows(heads_back(value_grad), level_offsets, stride, 0.0)
    return (attended.reshape(length, width),
            grad_q_sum.reshape(length, width).astype(jnp.bfloat16),
            grad_k_sum.reshape(length, width).astype(jnp.bfloat16),
            grad_v_sum.reshape(length, width).astype(jnp.bfloat16))
```

```python
import functools
import math

import jax
import jax.numpy as jnp
from jax import lax
from jax.experimental import pallas as pl
from jax.experimental.pallas import tpu as pltpu
from jax.sharding import PartitionSpec as P

HDIM = 48
LEVELS = 8


def swapped(shard, axis, bit):
    return lax.ppermute(shard, axis, [(i, i ^ 1 << bit) for i in range(lax.axis_size(axis))])


def pick_rows(values, level_offsets, stride):
    if stride == 1:
        return values
    length, head_count = (values.shape[0], values.shape[1])
    trailing = values.shape[2:]
    grouped = values.reshape((length // stride, stride, head_count) + trailing)
    marks = jnp.arange(stride, dtype=jnp.int32)[:, None] == level_offsets[None, :]
    marks = marks.reshape((1, stride, head_count) + (1,) * len(trailing))
    kept = jnp.where(marks, grouped, jnp.zeros((), values.dtype))
    return jnp.sum(kept, axis=1, dtype=values.dtype)


def spread_rows(values, level_offsets, stride, fill):
    count, head_count = (values.shape[0], values.shape[1])
    trailing = values.shape[2:]
    marks = jnp.arange(stride, dtype=jnp.int32)[:, None] == level_offsets[None, :]
    marks = marks.reshape((1, stride, head_count) + (1,) * len(trailing))
    placed = jnp.where(marks, values[:, None], jnp.asarray(fill, values.dtype))
    return placed.reshape((count * stride, head_count) + trailing)


def pair_bits(count):
    return list(range(count))


def send_pairs(block_rows, bit_no):
    return swapped(block_rows, "seq", bit_no)


def send_partials(block_rows, bit_no):
    return swapped(block_rows.astype(jnp.bfloat16), "seq", bit_no).astype(block_rows.dtype)


def double_up(block_rows, bit_list, sender):
    position = lax.axis_index("seq")
    for bit_no in bit_list:
        partner_rows = sender(block_rows, bit_no)
        upper_half = position // 2**bit_no % 2 == 1
        block_rows = jnp.where(
            upper_half,
            jnp.concatenate([partner_rows, block_rows], 0),
            jnp.concatenate([block_rows, partner_rows], 0),
        )
    return block_rows


def halve_down(buffer, bit_list, sender):
    position = lax.axis_index("seq")
    for bit_no in reversed(bit_list):
        half_rows = buffer.shape[0] // 2
        lower_part, upper_part = (buffer[:half_rows], buffer[half_rows:])
        upper_half = position // 2**bit_no % 2 == 1
        kept_half = jnp.where(upper_half, upper_part, lower_part)
        given_half = jnp.where(upper_half, lower_part, upper_part)
        buffer = kept_half + sender(given_half, bit_no)
    return buffer


def head_blocks(heads_here):
    block_width = min(heads_here, 4)
    return [
        (first, min(first + block_width, heads_here)) for first in range(0, heads_here, block_width)
    ]


def forward_level(query_seg, key_seg, value_seg, factor):
    largest_list, total_list, summed_list = ([], [], [])
    for first, last in head_blocks(query_seg.shape[2]):
        scores = (
            jnp.einsum(
                "nihd,njhd->nhij",
                query_seg[:, :, first:last],
                key_seg[:, :, first:last],
                preferred_element_type=jnp.float32,
            )
            * factor
        )
        largest = jnp.max(scores, axis=3)
        powers = jnp.exp(scores - largest[..., None])
        largest_list.append(largest)
        total_list.append(jnp.sum(powers, axis=3))
        summed_list.append(
            jnp.einsum(
                "nhij,njhd->nihd",
                powers.astype(jnp.bfloat16),
                value_seg[:, :, first:last],
                preferred_element_type=jnp.float32,
            )
        )
    return (
        jnp.concatenate(largest_list, 1),
        jnp.concatenate(total_list, 1),
        jnp.concatenate(summed_list, 2),
    )


def level_grads(query_seg, key_seg, value_seg, outgrad_seg, total_seg, dot_seg, factor):
    query_list, key_list, value_list = ([], [], [])
    for first, last in head_blocks(query_seg.shape[2]):
        query_part = query_seg[:, :, first:last]
        key_block = key_seg[:, :, first:last]
        outgrad_part = outgrad_seg[:, :, first:last]
        scores = (
            jnp.einsum("nihd,njhd->nhij", query_part, key_block, preferred_element_type=jnp.float32)
            * factor
        )
        weights = jnp.exp(scores - total_seg[:, first:last, :, None])
        grad_prob = jnp.einsum(
            "nihd,njhd->nhij",
            outgrad_part,
            value_seg[:, :, first:last],
            preferred_element_type=jnp.float32,
        )
        grad_score = (weights * (grad_prob - dot_seg[:, first:last, :, None])).astype(jnp.bfloat16)
        query_list.append(
            jnp.einsum("nhij,njhd->nihd", grad_score, key_block, preferred_element_type=jnp.float32)
            * factor
        )
        key_list.append(
            jnp.einsum(
                "nhij,nihd->njhd", grad_score, query_part, preferred_element_type=jnp.float32
            )
            * factor
        )
        value_list.append(
            jnp.einsum(
                "nhij,nihd->njhd",
                weights.astype(jnp.bfloat16),
                outgrad_part,
                preferred_element_type=jnp.float32,
            )
        )
    query_grad = jnp.concatenate(query_list, 2)
    key_grad = jnp.concatenate(key_list, 2)
    value_grad = jnp.concatenate(value_list, 2)
    return (query_grad, key_grad, value_grad)


def general_body(queries, key_rows, value_rows, grad_out, offsets):
    row_count = queries.shape[0]
    width_here = queries.shape[1]
    heads_here = width_here // HDIM
    factor = HDIM ** (-0.5)
    seq_count = lax.axis_size("seq")
    segment = row_count * seq_count // 2 ** (LEVELS - 1)
    head_first = lax.axis_index("head") * heads_here
    offsets_here = lax.dynamic_slice_in_dim(offsets, head_first, heads_here, 1)
    query_all = queries.reshape(row_count, heads_here, HDIM)
    key_all = key_rows.reshape(row_count, heads_here, HDIM)
    value_all = value_rows.reshape(row_count, heads_here, HDIM)
    outgrad_all = grad_out.reshape(row_count, heads_here, HDIM)
    levels_kept = []
    for level_no in range(LEVELS):
        stride = 2**level_no
        seg_span = segment * stride
        picked = row_count // stride
        level_offsets = offsets_here[level_no]
        query_lev = pick_rows(query_all, level_offsets, stride)
        key_lev = pick_rows(key_all, level_offsets, stride)
        value_lev = pick_rows(value_all, level_offsets, stride)
        if seg_span <= row_count:
            pieces = row_count // seg_span
            bit_list = []
            query_seg = query_lev.reshape(pieces, segment, heads_here, HDIM)
            key_seg = key_lev.reshape(pieces, segment, heads_here, HDIM)
            value_seg = value_lev.reshape(pieces, segment, heads_here, HDIM)
        else:
            group_size = seg_span // row_count
            packed = jnp.concatenate(
                [key_lev.reshape(picked, width_here), value_lev.reshape(picked, width_here)], 1
            )
            if group_size == seq_count:
                bit_list = list(range(group_size.bit_length() - 1))
                gathered = lax.all_gather(packed, "seq", axis=0, tiled=True)
            else:
                bit_list = pair_bits(group_size.bit_length() - 1)
                gathered = double_up(packed, bit_list, send_pairs)
            query_seg = query_lev.reshape(1, picked, heads_here, HDIM)
            key_seg = gathered[:, :width_here].reshape(1, segment, heads_here, HDIM)
            value_seg = gathered[:, width_here:].reshape(1, segment, heads_here, HDIM)
        largest, totals, summed = forward_level(query_seg, key_seg, value_seg, factor)
        level_max = spread_rows(
            jnp.transpose(largest, (0, 2, 1)).reshape(picked, heads_here),
            level_offsets,
            stride,
            -jnp.inf,
        )
        level_total = spread_rows(
            jnp.transpose(totals, (0, 2, 1)).reshape(picked, heads_here), level_offsets, stride, 0.0
        )
        level_sum = spread_rows(
            summed.reshape(picked, heads_here, HDIM), level_offsets, stride, 0.0
        )
        if level_no == 0:
            running_max, running_total, running_sum = (level_max, level_total, level_sum)
        else:
            newest_max = jnp.maximum(running_max, level_max)
            old_scale = jnp.exp(running_max - newest_max)
            new_scale = jnp.exp(level_max - newest_max)
            running_total = running_total * old_scale + level_total * new_scale
            running_sum = running_sum * old_scale[..., None] + level_sum * new_scale[..., None]
            running_max = newest_max
        levels_kept.append(
            (
                stride,
                level_offsets,
                seg_span,
                bit_list,
                query_lev,
                key_lev,
                value_lev,
                query_seg,
                key_seg,
                value_seg,
            )
        )
    attended = (running_sum / running_total[..., None]).astype(jnp.bfloat16)
    log_total = running_max + jnp.log(running_total)
    dot_rows = jnp.sum(outgrad_all.astype(jnp.float32) * attended.astype(jnp.float32), axis=2)
    grad_q_sum = jnp.zeros((row_count, heads_here, HDIM), jnp.float32)
    grad_k_sum = jnp.zeros((row_count, heads_here, HDIM), jnp.float32)
    grad_v_sum = jnp.zeros((row_count, heads_here, HDIM), jnp.float32)
    for (
        stride,
        level_offsets,
        seg_span,
        bit_list,
        query_lev,
        key_lev,
        value_lev,
        query_seg,
        key_seg,
        value_seg,
    ) in levels_kept:
        picked = row_count // stride
        outgrad_lev = pick_rows(outgrad_all, level_offsets, stride)
        total_lev = pick_rows(log_total, level_offsets, stride)
        dot_lev = pick_rows(dot_rows, level_offsets, stride)
        pieces = query_seg.shape[0]
        rows_each = query_seg.shape[1]
        outgrad_seg = outgrad_lev.reshape(pieces, rows_each, heads_here, HDIM)
        total_seg = jnp.transpose(total_lev.reshape(pieces, rows_each, heads_here), (0, 2, 1))
        dot_seg = jnp.transpose(dot_lev.reshape(pieces, rows_each, heads_here), (0, 2, 1))
        if seg_span <= row_count:
            grad_query_lev, key_part, value_part = level_grads(
                query_seg, key_seg, value_seg, outgrad_seg, total_seg, dot_seg, factor
            )
            key_grad = key_part.reshape(picked, heads_here, HDIM)
            value_grad = value_part.reshape(picked, heads_here, HDIM)
        else:
            grad_query_lev, key_part, value_part = level_grads(
                query_seg, key_seg, value_seg, outgrad_seg, total_seg, dot_seg, factor
            )
            packed = jnp.concatenate(
                [key_part.reshape(segment, width_here), value_part.reshape(segment, width_here)], 1
            )
            own_rows = halve_down(packed, bit_list, send_partials)
            key_grad = own_rows[:, :width_here].reshape(picked, heads_here, HDIM)
            value_grad = own_rows[:, width_here:].reshape(picked, heads_here, HDIM)
        grad_q_sum = grad_q_sum + spread_rows(
            grad_query_lev.reshape(picked, heads_here, HDIM), level_offsets, stride, 0.0
        )
        grad_k_sum = grad_k_sum + spread_rows(key_grad, level_offsets, stride, 0.0)
        grad_v_sum = grad_v_sum + spread_rows(value_grad, level_offsets, stride, 0.0)
    return (
        attended.reshape(row_count, width_here),
        grad_q_sum.reshape(row_count, width_here).astype(jnp.bfloat16),
        grad_k_sum.reshape(row_count, width_here).astype(jnp.bfloat16),
        grad_v_sum.reshape(row_count, width_here).astype(jnp.bfloat16),
    )


SEG = 8
LOCAL = 5
NEG = -1e30
NN = (((1,), (0,)), ((), ()))
NT = (((1,), (1,)), ((), ()))


def mm(lhs, rhs, dims=NN):
    return lax.dot_general(lhs, rhs, dims, preferred_element_type=jnp.float32)


def flipped(block):
    return block.astype(jnp.float32).T.astype(jnp.bfloat16)


def window(head_no):
    first = head_no * HDIM
    return first // 128 * 128, -(-(first + HDIM) // 128) * 128


def zero_extended(rows, head_no):
    low, high = window(head_no)
    first = head_no * HDIM
    parts = []
    if first > low:
        parts.append(jnp.zeros((first - low, rows.shape[1]), rows.dtype))
    parts.append(rows[first : first + HDIM])
    if high > first + HDIM:
        parts.append(jnp.zeros((high - first - HDIM, rows.shape[1]), rows.dtype))
    return parts[0] if len(parts) == 1 else jnp.concatenate(parts, 0)


def kernel(
    seq_count, heads, offs, q_ref, k_ref, v_ref, g_ref,
    att_ref, dq_ref, dk_ref, dv_ref,
    buf5, buf6, buf7, stat, build, slots, e_scr, dp_scr,
    send5, recv5, send6, recv6, send7, recv7, send_st, recv_st,
):
    me = lax.axis_index("seq")
    f32, bf16 = jnp.float32, jnp.bfloat16
    factor = HDIM ** (-0.5)
    factor2 = factor * math.log2(math.e)
    rows = q_ref.shape[0]
    width = q_ref.shape[1]
    head_first = lax.axis_index("head") * heads

    def peer(dist):
        low = lax.rem(me, 2)
        mid = lax.rem(me // 2, 2)
        top = me // 4
        b0, b1, b2 = dist & 1, dist >> 1 & 1, dist >> 2
        low = 1 - low if b0 else low
        mid = 1 - mid if b1 else mid
        top = 1 - top if b2 else top
        return top * 4 + mid * 2 + low

    barrier = pltpu.get_barrier_semaphore()
    for dist in range(1, seq_count):
        pl.semaphore_signal(
            barrier, inc=1, device_id={"seq": peer(dist)}, device_id_type=pl.DeviceIdType.MESH
        )

    off = [[offs[lev, head_first + h] for h in range(heads)] for lev in range(LEVELS)]
    refs = (q_ref, k_ref, v_ref, g_ref)

    slot_no = lax.broadcasted_iota(jnp.int32, (SEG, rows), 0)
    lane_no = lax.broadcasted_iota(jnp.int32, (SEG, rows), 1)
    picks = []
    for h in range(heads):
        target = jnp.where(
            slot_no < 4,
            slot_no * 32 + off[5][h],
            jnp.where(slot_no < 6, (slot_no - 4) * 64 + off[6][h], off[7][h]),
        )
        target = jnp.where(slot_no == 7, -1, target)
        picks.append(target == lane_no)
    chosen = jnp.concatenate([jnp.where(p, 1.0, 0.0) for p in picks], 0).astype(bf16)
    col_head = lax.broadcasted_iota(jnp.int32, (SEG, width), 1)
    for a in range(4):
        got = mm(chosen, refs[a][...])
        own = jnp.zeros((SEG, width), f32)
        for h in range(heads):
            inside = (col_head >= h * HDIM) & (col_head < (h + 1) * HDIM)
            own = jnp.where(inside, got[h * SEG : (h + 1) * SEG], own)
        build[4 * a : 4 * a + 4, :] = own[0:4]
        build[16 + 2 * a : 18 + 2 * a, :] = own[4:6]
        for c in range(3):
            build[32 + 4 * a + c : 33 + 4 * a + c, 0:128] = own[6:7, 128 * c : 128 * c + 128]
        build[35 + 4 * a : 36 + 4 * a, 0:128] = jnp.zeros((1, 128), f32)
    build[24:32, :] = jnp.zeros((8, width), f32)
    buf5[0] = build[0:16, :].astype(bf16)
    buf6[0] = build[16:32, :].astype(bf16)
    buf7[0] = build[32:48, 0:128].astype(bf16)

    pl.semaphore_wait(barrier, seq_count - 1)

    def remote(buf, send, recv, dist):
        return pltpu.make_async_remote_copy(
            src_ref=buf.at[0],
            dst_ref=buf.at[dist],
            send_sem=send.at[dist],
            recv_sem=recv.at[dist],
            device_id={"seq": peer(dist)},
            device_id_type=pl.DeviceIdType.MESH,
        )

    first = [remote(buf7, send7, recv7, d) for d in (7, 6, 5, 4, 3, 2, 1)]
    first += [remote(buf6, send6, recv6, d) for d in (3, 2, 1)]
    first += [remote(buf5, send5, recv5, 1)]
    for copy in first:
        copy.start()

    qt, kt, vt, gt = [flipped(r[...]) for r in refs]

    feat_no = lax.broadcasted_iota(jnp.int32, (32, rows), 0)
    pos = lax.broadcasted_iota(jnp.int32, (32, rows), 1)
    feats = []
    starts = (0, 16, 24, 28, 30)
    place = feat_no - 0
    seg_of = pos // 8
    rest = pos & 0
    for lev in range(1, LOCAL):
        past = feat_no >= starts[lev]
        place = jnp.where(past, feat_no - starts[lev], place)
        seg_of = jnp.where(past, pos // (8 << lev), seg_of)
        rest = jnp.where(past, pos & ((1 << lev) - 1), rest)
    in_seg = (place == seg_of) & (feat_no < 31)
    for h in range(heads):
        wanted = jnp.where(feat_no >= 16, off[1][h], 0)
        for lev in range(2, LOCAL):
            wanted = jnp.where(feat_no >= starts[lev], off[lev][h], wanted)
        feats.append(jnp.where(in_seg & (rest == wanted), 1.0, 0.0))
    feat_rows = [
        jnp.concatenate(feats[4 * b : 4 * b + 4], 0).T.astype(bf16) for b in range(heads // 4)
    ]
    tops = []
    counts = []
    for h in range(heads):
        low, high = window(h)
        before = 32 * (h % 4)
        parts = [jnp.zeros((before, rows), bf16)] if before else []
        parts.append(feats[h].astype(bf16))
        if before < 96:
            parts.append(jnp.zeros((96 - before, rows), bf16))
        count = mm(feat_rows[h // 4], jnp.concatenate(parts, 0))
        score = mm(k_ref[:, low:high], zero_extended(qt, h)) * factor2
        score = jnp.where(count > 0, score, NEG)
        top = jnp.max(score, axis=0, keepdims=True)
        tops.append(top)
        e_scr[h] = count * jnp.exp2(score - top)
        dp_scr[h] = mm(v_ref[:, low:high], zero_extended(gt, h))

    for copy in first:
        copy.wait()
    kinds = []
    for a in range(4):
        for d in range(2):
            slots[4 * d : 4 * d + 4, :] = buf5[d].astype(f32)[4 * a : 4 * a + 4]
        for d in range(4):
            slots[8 + 2 * d : 10 + 2 * d, :] = buf6[d].astype(f32)[2 * a : 2 * a + 2]
        for d in range(8):
            for c in range(3):
                slots[16 + d : 17 + d, 128 * c : 128 * c + 128] = buf7[d].astype(f32)[
                    4 * a + c : 4 * a + c + 1
                ]
        slots[24:32, :] = jnp.zeros((8, width), f32)
        kinds.append(slots[...])
    q_sl, k_sl, v_sl, g_sl = [x.astype(bf16) for x in kinds]
    q_st, k_st, v_st, g_st = [x.T.astype(bf16) for x in kinds]

    row32 = lax.broadcasted_iota(jnp.int32, (32, rows), 0)
    lane32 = lax.broadcasted_iota(jnp.int32, (32, rows), 1)
    span = jnp.where(row32 < 8, 31, jnp.where(row32 < 16, 63, 127))
    rest32 = lane32 & span
    held = []
    parts_far = []
    delta_rows = []
    inv_rows = []
    note = jnp.zeros((SEG, 128), f32)
    lane8 = lax.broadcasted_iota(jnp.int32, (SEG, 128), 1)
    for h in range(heads):
        low, high = window(h)
        cut = slice(h * HDIM, (h + 1) * HDIM)
        wanted = jnp.where(row32 < 8, off[5][h], jnp.where(row32 < 16, off[6][h], off[7][h]))
        inside = (rest32 == wanted) & (row32 < 24)
        held.append(inside)
        far = mm(k_sl[:, low:high], zero_extended(qt, h)) * factor2
        far = jnp.where(inside, far, NEG)
        top = jnp.maximum(tops[h], jnp.max(far, axis=0, keepdims=True))
        e_far = jnp.exp2(far - top)
        shrink = jnp.exp2(tops[h] - top)
        near = e_scr[h]
        total = jnp.sum(near, axis=0, keepdims=True) * shrink + jnp.sum(
            e_far, axis=0, keepdims=True
        )
        inv = 1.0 / total
        near = near * (shrink * inv)
        e_far = e_far * inv
        e_scr[h] = near
        out = mm(vt[cut], near.astype(bf16)) + mm(v_st[cut], e_far.astype(bf16))
        out = out.astype(bf16).astype(f32)
        att_ref[cut, :] = out
        delta = jnp.sum(out * gt[cut].astype(f32), axis=0, keepdims=True)
        delta_rows.append(delta)
        parts_far.append(e_far)
        lse = top + jnp.log2(total)
        lse_col = jnp.sum(jnp.where(picks[h], lse, 0.0), axis=1, keepdims=True)
        delta_col = jnp.sum(jnp.where(picks[h], delta, 0.0), axis=1, keepdims=True)
        note = jnp.where(lane8 == h, lse_col, note)
        note = jnp.where(lane8 == heads + h, delta_col, note)
    stat[0] = note
    second = [remote(stat, send_st, recv_st, d) for d in (7, 6, 5, 4, 3, 2, 1)]
    for copy in second:
        copy.start()

    near_k, near_v, far_s, far_p = [], [], [], []
    for h in range(heads):
        low, high = window(h)
        cut = slice(h * HDIM, (h + 1) * HDIM)
        near = e_scr[h]
        ds = (near * (dp_scr[h] - delta_rows[h])).astype(bf16)
        dp_far = mm(v_sl[:, low:high], zero_extended(gt, h))
        ds_far = (parts_far[h] * (dp_far - delta_rows[h])).astype(bf16)
        dq_ref[cut, :] = (mm(kt[cut], ds) + mm(k_st[cut], ds_far)) * factor
        dk_ref[cut, :] = mm(qt[cut], ds, NT)
        dv_ref[cut, :] = mm(gt[cut], near.astype(bf16), NT)
        far_s.append(mm(q_sl[:, low:high], zero_extended(kt, h)) * factor2)
        far_p.append(mm(g_sl[:, low:high], zero_extended(vt, h)))

    for copy in second:
        copy.wait()
    for d in range(2):
        slots[4 * d : 4 * d + 4, 0:128] = stat[d, 0:4]
    for d in range(4):
        slots[8 + 2 * d : 10 + 2 * d, 0:128] = stat[d, 4:6]
    for d in range(8):
        slots[16 + d : 17 + d, 0:128] = stat[d, 6:7]
    notes = slots[:, 0:128]
    for h in range(heads):
        cut = slice(h * HDIM, (h + 1) * HDIM)
        lse = notes[:, h : h + 1]
        delta = notes[:, heads + h : heads + h + 1]
        prob = jnp.exp2(jnp.where(held[h], far_s[h] - lse, NEG))
        ds = (prob * (far_p[h] - delta)).astype(bf16)
        dk_ref[cut, :] = (dk_ref[cut, :] + mm(q_st[cut], ds)) * factor
        dv_ref[cut, :] = dv_ref[cut, :] + mm(g_st[cut], prob.astype(bf16))


def small_body(queries, key_rows, value_rows, grad_out, offsets):
    rows, width = queries.shape
    heads = width // HDIM
    seq_count = lax.axis_size("seq")
    vmem = pl.BlockSpec(memory_space=pltpu.VMEM)
    dma = pltpu.SemaphoreType.DMA
    outs = pl.pallas_call(
        functools.partial(kernel, seq_count, heads),
        out_shape=[jax.ShapeDtypeStruct((width, rows), jnp.float32)] * 4,
        in_specs=[pl.BlockSpec(memory_space=pltpu.SMEM)] + [vmem] * 4,
        out_specs=[vmem] * 4,
        scratch_shapes=[
            pltpu.VMEM((2, 16, width), jnp.bfloat16),
            pltpu.VMEM((4, 16, width), jnp.bfloat16),
            pltpu.VMEM((8, 16, 128), jnp.bfloat16),
            pltpu.VMEM((8, SEG, 128), jnp.float32),
            pltpu.VMEM((48, width), jnp.float32),
            pltpu.VMEM((32, width), jnp.float32),
            pltpu.VMEM((heads, rows, rows), jnp.float32),
            pltpu.VMEM((heads, rows, rows), jnp.float32),
            dma((2,)), dma((2,)), dma((4,)), dma((4,)),
            dma((8,)), dma((8,)), dma((8,)), dma((8,)),
        ],
        compiler_params=pltpu.CompilerParams(
            collective_id=0, has_side_effects=True, vmem_limit_bytes=32 * 2**20
        ),
    )(offsets, queries, key_rows, value_rows, grad_out)
    return tuple(x.T.astype(jnp.bfloat16) for x in outs)


def body(queries, key_rows, value_rows, grad_out, offsets):
    rows, width = queries.shape
    seq_count = lax.axis_size("seq")
    if seq_count == 8 and rows == 128 and width == 8 * HDIM:
        return small_body(queries, key_rows, value_rows, grad_out, offsets)
    return general_body(queries, key_rows, value_rows, grad_out, offsets)


def solution(mesh):
    placed = (
        P(("groups", "seq"), "head"),
        P(("groups", "seq"), "head"),
        P(("groups", "seq"), "head"),
        P(("groups", "seq"), "head"),
        P(),
    )
    return jax.shard_map(
        body,
        mesh=mesh,
        in_specs=placed,
        out_specs=(
            P(("groups", "seq"), "head"),
            P(("groups", "seq"), "head"),
            P(("groups", "seq"), "head"),
            P(("groups", "seq"), "head"),
        ),
        check_vma=False,
    )
```

```python
import functools
import math

import jax
import jax.numpy as jnp
from jax import lax
from jax.experimental import pallas as pl
from jax.experimental.pallas import tpu as pltpu
from jax.sharding import PartitionSpec as P

HDIM = 48
LEVELS = 8


def swapped(shard, axis, bit):
    return lax.ppermute(shard, axis, [(i, i ^ 1 << bit) for i in range(lax.axis_size(axis))])


def pick_rows(values, level_offsets, stride):
    if stride == 1:
        return values
    length, head_count = (values.shape[0], values.shape[1])
    trailing = values.shape[2:]
    grouped = values.reshape((length // stride, stride, head_count) + trailing)
    marks = jnp.arange(stride, dtype=jnp.int32)[:, None] == level_offsets[None, :]
    marks = marks.reshape((1, stride, head_count) + (1,) * len(trailing))
    kept = jnp.where(marks, grouped, jnp.zeros((), values.dtype))
    return jnp.sum(kept, axis=1, dtype=values.dtype)


def spread_rows(values, level_offsets, stride, fill):
    count, head_count = (values.shape[0], values.shape[1])
    trailing = values.shape[2:]
    marks = jnp.arange(stride, dtype=jnp.int32)[:, None] == level_offsets[None, :]
    marks = marks.reshape((1, stride, head_count) + (1,) * len(trailing))
    placed = jnp.where(marks, values[:, None], jnp.asarray(fill, values.dtype))
    return placed.reshape((count * stride, head_count) + trailing)


def pair_bits(count):
    return list(range(count))


def send_pairs(block_rows, bit_no):
    return swapped(block_rows, "seq", bit_no)


def send_partials(block_rows, bit_no):
    return swapped(block_rows.astype(jnp.bfloat16), "seq", bit_no).astype(block_rows.dtype)


def double_up(block_rows, bit_list, sender):
    position = lax.axis_index("seq")
    for bit_no in bit_list:
        partner_rows = sender(block_rows, bit_no)
        upper_half = position // 2**bit_no % 2 == 1
        block_rows = jnp.where(
            upper_half,
            jnp.concatenate([partner_rows, block_rows], 0),
            jnp.concatenate([block_rows, partner_rows], 0),
        )
    return block_rows


def halve_down(buffer, bit_list, sender):
    position = lax.axis_index("seq")
    for bit_no in reversed(bit_list):
        half_rows = buffer.shape[0] // 2
        lower_part, upper_part = (buffer[:half_rows], buffer[half_rows:])
        upper_half = position // 2**bit_no % 2 == 1
        kept_half = jnp.where(upper_half, upper_part, lower_part)
        given_half = jnp.where(upper_half, lower_part, upper_part)
        buffer = kept_half + sender(given_half, bit_no)
    return buffer


def head_blocks(heads_here):
    block_width = min(heads_here, 4)
    return [
        (first, min(first + block_width, heads_here)) for first in range(0, heads_here, block_width)
    ]


def forward_level(query_seg, key_seg, value_seg, factor):
    largest_list, total_list, summed_list = ([], [], [])
    for first, last in head_blocks(query_seg.shape[2]):
        scores = (
            jnp.einsum(
                "nihd,njhd->nhij",
                query_seg[:, :, first:last],
                key_seg[:, :, first:last],
                preferred_element_type=jnp.float32,
            )
            * factor
        )
        largest = jnp.max(scores, axis=3)
        powers = jnp.exp(scores - largest[..., None])
        largest_list.append(largest)
        total_list.append(jnp.sum(powers, axis=3))
        summed_list.append(
            jnp.einsum(
                "nhij,njhd->nihd",
                powers.astype(jnp.bfloat16),
                value_seg[:, :, first:last],
                preferred_element_type=jnp.float32,
            )
        )
    return (
        jnp.concatenate(largest_list, 1),
        jnp.concatenate(total_list, 1),
        jnp.concatenate(summed_list, 2),
    )


def level_grads(query_seg, key_seg, value_seg, outgrad_seg, total_seg, dot_seg, factor):
    query_list, key_list, value_list = ([], [], [])
    for first, last in head_blocks(query_seg.shape[2]):
        query_part = query_seg[:, :, first:last]
        key_block = key_seg[:, :, first:last]
        outgrad_part = outgrad_seg[:, :, first:last]
        scores = (
            jnp.einsum("nihd,njhd->nhij", query_part, key_block, preferred_element_type=jnp.float32)
            * factor
        )
        weights = jnp.exp(scores - total_seg[:, first:last, :, None])
        grad_prob = jnp.einsum(
            "nihd,njhd->nhij",
            outgrad_part,
            value_seg[:, :, first:last],
            preferred_element_type=jnp.float32,
        )
        grad_score = (weights * (grad_prob - dot_seg[:, first:last, :, None])).astype(jnp.bfloat16)
        query_list.append(
            jnp.einsum("nhij,njhd->nihd", grad_score, key_block, preferred_element_type=jnp.float32)
            * factor
        )
        key_list.append(
            jnp.einsum(
                "nhij,nihd->njhd", grad_score, query_part, preferred_element_type=jnp.float32
            )
            * factor
        )
        value_list.append(
            jnp.einsum(
                "nhij,nihd->njhd",
                weights.astype(jnp.bfloat16),
                outgrad_part,
                preferred_element_type=jnp.float32,
            )
        )
    query_grad = jnp.concatenate(query_list, 2)
    key_grad = jnp.concatenate(key_list, 2)
    value_grad = jnp.concatenate(value_list, 2)
    return (query_grad, key_grad, value_grad)


def general_body(queries, key_rows, value_rows, grad_out, offsets):
    row_count = queries.shape[0]
    width_here = queries.shape[1]
    heads_here = width_here // HDIM
    factor = HDIM ** (-0.5)
    seq_count = lax.axis_size("seq")
    segment = row_count * seq_count // 2 ** (LEVELS - 1)
    head_first = lax.axis_index("head") * heads_here
    offsets_here = lax.dynamic_slice_in_dim(offsets, head_first, heads_here, 1)
    query_all = queries.reshape(row_count, heads_here, HDIM)
    key_all = key_rows.reshape(row_count, heads_here, HDIM)
    value_all = value_rows.reshape(row_count, heads_here, HDIM)
    outgrad_all = grad_out.reshape(row_count, heads_here, HDIM)
    levels_kept = []
    for level_no in range(LEVELS):
        stride = 2**level_no
        seg_span = segment * stride
        picked = row_count // stride
        level_offsets = offsets_here[level_no]
        query_lev = pick_rows(query_all, level_offsets, stride)
        key_lev = pick_rows(key_all, level_offsets, stride)
        value_lev = pick_rows(value_all, level_offsets, stride)
        if seg_span <= row_count:
            pieces = row_count // seg_span
            bit_list = []
            query_seg = query_lev.reshape(pieces, segment, heads_here, HDIM)
            key_seg = key_lev.reshape(pieces, segment, heads_here, HDIM)
            value_seg = value_lev.reshape(pieces, segment, heads_here, HDIM)
        else:
            group_size = seg_span // row_count
            packed = jnp.concatenate(
                [key_lev.reshape(picked, width_here), value_lev.reshape(picked, width_here)], 1
            )
            if group_size == seq_count:
                bit_list = list(range(group_size.bit_length() - 1))
                gathered = lax.all_gather(packed, "seq", axis=0, tiled=True)
            else:
                bit_list = pair_bits(group_size.bit_length() - 1)
                gathered = double_up(packed, bit_list, send_pairs)
            query_seg = query_lev.reshape(1, picked, heads_here, HDIM)
            key_seg = gathered[:, :width_here].reshape(1, segment, heads_here, HDIM)
            value_seg = gathered[:, width_here:].reshape(1, segment, heads_here, HDIM)
        largest, totals, summed = forward_level(query_seg, key_seg, value_seg, factor)
        level_max = spread_rows(
            jnp.transpose(largest, (0, 2, 1)).reshape(picked, heads_here),
            level_offsets,
            stride,
            -jnp.inf,
        )
        level_total = spread_rows(
            jnp.transpose(totals, (0, 2, 1)).reshape(picked, heads_here), level_offsets, stride, 0.0
        )
        level_sum = spread_rows(
            summed.reshape(picked, heads_here, HDIM), level_offsets, stride, 0.0
        )
        if level_no == 0:
            running_max, running_total, running_sum = (level_max, level_total, level_sum)
        else:
            newest_max = jnp.maximum(running_max, level_max)
            old_scale = jnp.exp(running_max - newest_max)
            new_scale = jnp.exp(level_max - newest_max)
            running_total = running_total * old_scale + level_total * new_scale
            running_sum = running_sum * old_scale[..., None] + level_sum * new_scale[..., None]
            running_max = newest_max
        levels_kept.append(
            (
                stride,
                level_offsets,
                seg_span,
                bit_list,
                query_lev,
                key_lev,
                value_lev,
                query_seg,
                key_seg,
                value_seg,
            )
        )
    attended = (running_sum / running_total[..., None]).astype(jnp.bfloat16)
    log_total = running_max + jnp.log(running_total)
    dot_rows = jnp.sum(outgrad_all.astype(jnp.float32) * attended.astype(jnp.float32), axis=2)
    grad_q_sum = jnp.zeros((row_count, heads_here, HDIM), jnp.float32)
    grad_k_sum = jnp.zeros((row_count, heads_here, HDIM), jnp.float32)
    grad_v_sum = jnp.zeros((row_count, heads_here, HDIM), jnp.float32)
    for (
        stride,
        level_offsets,
        seg_span,
        bit_list,
        query_lev,
        key_lev,
        value_lev,
        query_seg,
        key_seg,
        value_seg,
    ) in levels_kept:
        picked = row_count // stride
        outgrad_lev = pick_rows(outgrad_all, level_offsets, stride)
        total_lev = pick_rows(log_total, level_offsets, stride)
        dot_lev = pick_rows(dot_rows, level_offsets, stride)
        pieces = query_seg.shape[0]
        rows_each = query_seg.shape[1]
        outgrad_seg = outgrad_lev.reshape(pieces, rows_each, heads_here, HDIM)
        total_seg = jnp.transpose(total_lev.reshape(pieces, rows_each, heads_here), (0, 2, 1))
        dot_seg = jnp.transpose(dot_lev.reshape(pieces, rows_each, heads_here), (0, 2, 1))
        if seg_span <= row_count:
            grad_query_lev, key_part, value_part = level_grads(
                query_seg, key_seg, value_seg, outgrad_seg, total_seg, dot_seg, factor
            )
            key_grad = key_part.reshape(picked, heads_here, HDIM)
            value_grad = value_part.reshape(picked, heads_here, HDIM)
        else:
            grad_query_lev, key_part, value_part = level_grads(
                query_seg, key_seg, value_seg, outgrad_seg, total_seg, dot_seg, factor
            )
            packed = jnp.concatenate(
                [key_part.reshape(segment, width_here), value_part.reshape(segment, width_here)], 1
            )
            own_rows = halve_down(packed, bit_list, send_partials)
            key_grad = own_rows[:, :width_here].reshape(picked, heads_here, HDIM)
            value_grad = own_rows[:, width_here:].reshape(picked, heads_here, HDIM)
        grad_q_sum = grad_q_sum + spread_rows(
            grad_query_lev.reshape(picked, heads_here, HDIM), level_offsets, stride, 0.0
        )
        grad_k_sum = grad_k_sum + spread_rows(key_grad, level_offsets, stride, 0.0)
        grad_v_sum = grad_v_sum + spread_rows(value_grad, level_offsets, stride, 0.0)
    return (
        attended.reshape(row_count, width_here),
        grad_q_sum.reshape(row_count, width_here).astype(jnp.bfloat16),
        grad_k_sum.reshape(row_count, width_here).astype(jnp.bfloat16),
        grad_v_sum.reshape(row_count, width_here).astype(jnp.bfloat16),
    )


SEG = 8
LOCAL = 5
NEG = -1e30
NN = (((1,), (0,)), ((), ()))
NT = (((1,), (1,)), ((), ()))


def mm(lhs, rhs, dims=NN):
    return lax.dot_general(lhs, rhs, dims, preferred_element_type=jnp.float32)


def flipped(block):
    return block.astype(jnp.bfloat16).T


def window(head_no):
    first = head_no * HDIM
    return first // 128 * 128, -(-(first + HDIM) // 128) * 128


def zero_extended(rows, head_no):
    low, high = window(head_no)
    first = head_no * HDIM
    parts = []
    if first > low:
        parts.append(jnp.zeros((first - low, rows.shape[1]), rows.dtype))
    parts.append(rows[first : first + HDIM])
    if high > first + HDIM:
        parts.append(jnp.zeros((high - first - HDIM, rows.shape[1]), rows.dtype))
    return parts[0] if len(parts) == 1 else jnp.concatenate(parts, 0)


def kernel(
    seq_count, heads, offs_hbm, q_hbm, k_hbm, v_hbm, g_hbm,
    att_out, dq_out, dk_out, dv_out,
    offs, q_ref, k_ref, v_ref, g_ref, att_ref, dq_ref, dk_ref, dv_ref, fetch,
    buf5, buf6, buf7, stat, build, slots, e_scr, dp_scr,
    send5, recv5, send6, recv6, send7, recv7, send_st, recv_st,
):
    me = lax.axis_index("seq")
    fetches = [
        pltpu.make_async_copy(here, there, fetch.at[i])
        for i, (here, there) in enumerate(
            ((offs_hbm, offs), (q_hbm, q_ref), (k_hbm, k_ref), (v_hbm, v_ref), (g_hbm, g_ref))
        )
    ]
    for copy in fetches:
        copy.start()
    f32, bf16 = jnp.float32, jnp.bfloat16
    factor = HDIM ** (-0.5)
    factor2 = factor * math.log2(math.e)
    rows = q_ref.shape[0]
    width = q_ref.shape[1]
    head_first = lax.axis_index("head") * heads

    def peer(dist):
        low = lax.rem(me, 2)
        mid = lax.rem(me // 2, 2)
        top = me // 4
        b0, b1, b2 = dist & 1, dist >> 1 & 1, dist >> 2
        low = 1 - low if b0 else low
        mid = 1 - mid if b1 else mid
        top = 1 - top if b2 else top
        return top * 4 + mid * 2 + low

    barrier = pltpu.get_barrier_semaphore()
    for dist in range(1, seq_count):
        pl.semaphore_signal(
            barrier, inc=1, device_id={"seq": peer(dist)}, device_id_type=pl.DeviceIdType.MESH
        )

    for copy in fetches:
        copy.wait()
    off = [[offs[lev, head_first + h] for h in range(heads)] for lev in range(LEVELS)]
    refs = (q_ref, k_ref, v_ref, g_ref)

    slot_no = lax.broadcasted_iota(jnp.int32, (SEG, rows), 0)
    lane_no = lax.broadcasted_iota(jnp.int32, (SEG, rows), 1)
    picks = []
    for h in range(heads):
        target = jnp.where(
            slot_no < 4,
            slot_no * 32 + off[5][h],
            jnp.where(slot_no < 6, (slot_no - 4) * 64 + off[6][h], off[7][h]),
        )
        target = jnp.where(slot_no == 7, -1, target)
        picks.append(target == lane_no)
    chosen = jnp.concatenate([jnp.where(p, 1.0, 0.0) for p in picks], 0).astype(bf16)
    col_head = lax.broadcasted_iota(jnp.int32, (SEG, width), 1)
    for a in range(4):
        got = mm(chosen, refs[a][...])
        own = jnp.zeros((SEG, width), f32)
        for h in range(heads):
            inside = (col_head >= h * HDIM) & (col_head < (h + 1) * HDIM)
            own = jnp.where(inside, got[h * SEG : (h + 1) * SEG], own)
        build[4 * a : 4 * a + 4, :] = own[0:4]
        build[16 + 2 * a : 18 + 2 * a, :] = own[4:6]
        for c in range(3):
            build[32 + 4 * a + c : 33 + 4 * a + c, 0:128] = own[6:7, 128 * c : 128 * c + 128]
        build[35 + 4 * a : 36 + 4 * a, 0:128] = jnp.zeros((1, 128), f32)
    build[24:32, :] = jnp.zeros((8, width), f32)
    buf5[0] = build[0:16, :].astype(bf16)
    buf6[0] = build[16:32, :].astype(bf16)
    buf7[0] = build[32:48, 0:128].astype(bf16)

    pl.semaphore_wait(barrier, seq_count - 1)

    def remote(buf, send, recv, dist):
        return pltpu.make_async_remote_copy(
            src_ref=buf.at[0],
            dst_ref=buf.at[dist],
            send_sem=send.at[dist],
            recv_sem=recv.at[dist],
            device_id={"seq": peer(dist)},
            device_id_type=pl.DeviceIdType.MESH,
        )

    first = [remote(buf7, send7, recv7, d) for d in (7, 6, 5, 4, 3, 2, 1)]
    first += [remote(buf6, send6, recv6, d) for d in (3, 2, 1)]
    first += [remote(buf5, send5, recv5, 1)]
    for copy in first:
        copy.start()

    qt, kt, vt, gt = [flipped(r[...]) for r in refs]

    feat_no = lax.broadcasted_iota(jnp.int32, (32, rows), 0)
    pos = lax.broadcasted_iota(jnp.int32, (32, rows), 1)
    feats = []
    starts = (0, 16, 24, 28, 30)
    place = feat_no - 0
    seg_of = pos // 8
    rest = pos & 0
    for lev in range(1, LOCAL):
        past = feat_no >= starts[lev]
        place = jnp.where(past, feat_no - starts[lev], place)
        seg_of = jnp.where(past, pos // (8 << lev), seg_of)
        rest = jnp.where(past, pos & ((1 << lev) - 1), rest)
    in_seg = (place == seg_of) & (feat_no < 31)
    for h in range(heads):
        wanted = jnp.where(feat_no >= 16, off[1][h], 0)
        for lev in range(2, LOCAL):
            wanted = jnp.where(feat_no >= starts[lev], off[lev][h], wanted)
        feats.append(jnp.where(in_seg & (rest == wanted), 1.0, 0.0))
    feat_rows = [
        jnp.concatenate(feats[4 * b : 4 * b + 4], 0).T.astype(bf16) for b in range(heads // 4)
    ]
    tops = []
    counts = []
    for h in range(heads):
        low, high = window(h)
        before = 32 * (h % 4)
        parts = [jnp.zeros((before, rows), bf16)] if before else []
        parts.append(feats[h].astype(bf16))
        if before < 96:
            parts.append(jnp.zeros((96 - before, rows), bf16))
        count = mm(feat_rows[h // 4], jnp.concatenate(parts, 0))
        score = mm(k_ref[:, low:high], zero_extended(qt, h)) * factor2
        score = jnp.where(count > 0, score, NEG)
        top = jnp.max(score, axis=0, keepdims=True)
        tops.append(top)
        e_scr[h] = count * jnp.exp2(score - top)
        dp_scr[h] = mm(v_ref[:, low:high], zero_extended(gt, h))

    for copy in first:
        copy.wait()
    kinds = []
    for a in range(4):
        for d in range(2):
            slots[4 * d : 4 * d + 4, :] = buf5[d].astype(f32)[4 * a : 4 * a + 4]
        for d in range(4):
            slots[8 + 2 * d : 10 + 2 * d, :] = buf6[d].astype(f32)[2 * a : 2 * a + 2]
        for d in range(8):
            for c in range(3):
                slots[16 + d : 17 + d, 128 * c : 128 * c + 128] = buf7[d].astype(f32)[
                    4 * a + c : 4 * a + c + 1
                ]
        slots[24:32, :] = jnp.zeros((8, width), f32)
        kinds.append(slots[...])
    q_sl, k_sl, v_sl, g_sl = [x.astype(bf16) for x in kinds]
    q_st, k_st, v_st, g_st = [x.T.astype(bf16) for x in kinds]

    row32 = lax.broadcasted_iota(jnp.int32, (32, rows), 0)
    lane32 = lax.broadcasted_iota(jnp.int32, (32, rows), 1)
    span = jnp.where(row32 < 8, 31, jnp.where(row32 < 16, 63, 127))
    rest32 = lane32 & span
    held = []
    parts_far = []
    delta_rows = []
    inv_rows = []
    note = jnp.zeros((SEG, 128), f32)
    lane8 = lax.broadcasted_iota(jnp.int32, (SEG, 128), 1)
    for h in range(heads):
        low, high = window(h)
        cut = slice(h * HDIM, (h + 1) * HDIM)
        wanted = jnp.where(row32 < 8, off[5][h], jnp.where(row32 < 16, off[6][h], off[7][h]))
        inside = (rest32 == wanted) & (row32 < 24)
        held.append(inside)
        far = mm(k_sl[:, low:high], zero_extended(qt, h)) * factor2
        far = jnp.where(inside, far, NEG)
        top = jnp.maximum(tops[h], jnp.max(far, axis=0, keepdims=True))
        e_far = jnp.exp2(far - top)
        shrink = jnp.exp2(tops[h] - top)
        near = e_scr[h]
        total = jnp.sum(near, axis=0, keepdims=True) * shrink + jnp.sum(
            e_far, axis=0, keepdims=True
        )
        inv = 1.0 / total
        near = near * (shrink * inv)
        e_far = e_far * inv
        e_scr[h] = near
        out = mm(vt[cut], near.astype(bf16)) + mm(v_st[cut], e_far.astype(bf16))
        out = out.astype(bf16).astype(f32)
        att_ref[cut, :] = out
        delta = jnp.sum(out * gt[cut].astype(f32), axis=0, keepdims=True)
        delta_rows.append(delta)
        parts_far.append(e_far)
        lse = top + jnp.log2(total)
        lse_col = jnp.sum(jnp.where(picks[h], lse, 0.0), axis=1, keepdims=True)
        delta_col = jnp.sum(jnp.where(picks[h], delta, 0.0), axis=1, keepdims=True)
        note = jnp.where(lane8 == h, lse_col, note)
        note = jnp.where(lane8 == heads + h, delta_col, note)
    stat[0] = note
    second = [remote(stat, send_st, recv_st, d) for d in (7, 6, 5, 4, 3, 2, 1)]
    for copy in second:
        copy.start()

    near_k, near_v, far_s, far_p = [], [], [], []
    for h in range(heads):
        low, high = window(h)
        cut = slice(h * HDIM, (h + 1) * HDIM)
        near = e_scr[h]
        ds = (near * (dp_scr[h] - delta_rows[h])).astype(bf16)
        dp_far = mm(v_sl[:, low:high], zero_extended(gt, h))
        ds_far = (parts_far[h] * (dp_far - delta_rows[h])).astype(bf16)
        dq_ref[cut, :] = (mm(kt[cut], ds) + mm(k_st[cut], ds_far)) * factor
        dk_ref[cut, :] = mm(qt[cut], ds, NT)
        dv_ref[cut, :] = mm(gt[cut], near.astype(bf16), NT)
        far_s.append(mm(q_sl[:, low:high], zero_extended(kt, h)) * factor2)
        far_p.append(mm(g_sl[:, low:high], zero_extended(vt, h)))

    att_out[...] = flipped(att_ref[...])
    dq_out[...] = flipped(dq_ref[...])
    for copy in second:
        copy.wait()
    for d in range(2):
        slots[4 * d : 4 * d + 4, 0:128] = stat[d, 0:4]
    for d in range(4):
        slots[8 + 2 * d : 10 + 2 * d, 0:128] = stat[d, 4:6]
    for d in range(8):
        slots[16 + d : 17 + d, 0:128] = stat[d, 6:7]
    notes = slots[:, 0:128]
    for h in range(heads):
        cut = slice(h * HDIM, (h + 1) * HDIM)
        lse = notes[:, h : h + 1]
        delta = notes[:, heads + h : heads + h + 1]
        prob = jnp.exp2(jnp.where(held[h], far_s[h] - lse, NEG))
        ds = (prob * (far_p[h] - delta)).astype(bf16)
        dk_ref[cut, :] = (dk_ref[cut, :] + mm(q_st[cut], ds)) * factor
        dv_ref[cut, :] = dv_ref[cut, :] + mm(g_st[cut], prob.astype(bf16))
    dk_out[...] = flipped(dk_ref[...])
    dv_out[...] = flipped(dv_ref[...])


def write_out(*refs):
    ends = refs[8]
    copies = [pltpu.make_async_copy(refs[i], refs[4 + i], ends.at[i]) for i in range(4)]
    for copy in copies:
        copy.start()
    for copy in copies:
        copy.wait()


def small_body(queries, key_rows, value_rows, grad_out, offsets):
    rows, width = queries.shape
    heads = width // HDIM
    seq_count = lax.axis_size("seq")
    hbm = pl.BlockSpec(memory_space=pltpu.HBM)
    vmem = pl.BlockSpec(memory_space=pltpu.VMEM)
    dma = pltpu.SemaphoreType.DMA
    outs = pl.pallas_call(
        functools.partial(kernel, seq_count, heads),
        out_shape=[jax.ShapeDtypeStruct((rows, width), jnp.bfloat16)] * 4,
        in_specs=[hbm] * 5,
        out_specs=[vmem] * 4,
        scratch_shapes=[
            pltpu.SMEM(offsets.shape, jnp.int32),
            *[pltpu.VMEM((rows, width), jnp.bfloat16)] * 4,
            *[pltpu.VMEM((width, rows), jnp.float32)] * 4,
            dma((5,)),
            pltpu.VMEM((2, 16, width), jnp.bfloat16),
            pltpu.VMEM((4, 16, width), jnp.bfloat16),
            pltpu.VMEM((8, 16, 128), jnp.bfloat16),
            pltpu.VMEM((8, SEG, 128), jnp.float32),
            pltpu.VMEM((48, width), jnp.float32),
            pltpu.VMEM((32, width), jnp.float32),
            pltpu.VMEM((heads, rows, rows), jnp.float32),
            pltpu.VMEM((heads, rows, rows), jnp.float32),
            dma((2,)), dma((2,)), dma((4,)), dma((4,)),
            dma((8,)), dma((8,)), dma((8,)), dma((8,)),
        ],
        compiler_params=pltpu.CompilerParams(
            collective_id=0, has_side_effects=True, vmem_limit_bytes=62 * 2**20
        ),
    )(offsets, queries, key_rows, value_rows, grad_out)
    return pl.pallas_call(
        write_out,
        out_shape=[jax.ShapeDtypeStruct((rows, width), jnp.bfloat16)] * 4,
        in_specs=[vmem] * 4,
        out_specs=[hbm] * 4,
        scratch_shapes=[dma((4,))],
    )(*outs)


def body(queries, key_rows, value_rows, grad_out, offsets):
    rows, width = queries.shape
    seq_count = lax.axis_size("seq")
    if seq_count == 8 and rows == 128 and width == 8 * HDIM:
        return small_body(queries, key_rows, value_rows, grad_out, offsets)
    return general_body(queries, key_rows, value_rows, grad_out, offsets)


def solution(mesh):
    placed = (
        P(("groups", "seq"), "head"),
        P(("groups", "seq"), "head"),
        P(("groups", "seq"), "head"),
        P(("groups", "seq"), "head"),
        P(),
    )
    return jax.shard_map(
        body,
        mesh=mesh,
        in_specs=placed,
        out_specs=(
            P(("groups", "seq"), "head"),
            P(("groups", "seq"), "head"),
            P(("groups", "seq"), "head"),
            P(("groups", "seq"), "head"),
        ),
        check_vma=False,
    )
```

```python
import functools
import math

import jax
import jax.numpy as jnp
from jax import lax
from jax.experimental import pallas as pl
from jax.experimental.pallas import tpu as pltpu
from jax.sharding import PartitionSpec as P

HDIM = 48
LEVELS = 8


def swapped(shard, axis, bit):
    return lax.ppermute(shard, axis, [(i, i ^ 1 << bit) for i in range(lax.axis_size(axis))])


def pick_rows(values, level_offsets, stride):
    if stride == 1:
        return values
    length, head_count = (values.shape[0], values.shape[1])
    trailing = values.shape[2:]
    grouped = values.reshape((length // stride, stride, head_count) + trailing)
    marks = jnp.arange(stride, dtype=jnp.int32)[:, None] == level_offsets[None, :]
    marks = marks.reshape((1, stride, head_count) + (1,) * len(trailing))
    kept = jnp.where(marks, grouped, jnp.zeros((), values.dtype))
    return jnp.sum(kept, axis=1, dtype=values.dtype)


def spread_rows(values, level_offsets, stride, fill):
    count, head_count = (values.shape[0], values.shape[1])
    trailing = values.shape[2:]
    marks = jnp.arange(stride, dtype=jnp.int32)[:, None] == level_offsets[None, :]
    marks = marks.reshape((1, stride, head_count) + (1,) * len(trailing))
    placed = jnp.where(marks, values[:, None], jnp.asarray(fill, values.dtype))
    return placed.reshape((count * stride, head_count) + trailing)


def pair_bits(count):
    return list(range(count))


def send_pairs(block_rows, bit_no):
    return swapped(block_rows, "seq", bit_no)


def send_partials(block_rows, bit_no):
    return swapped(block_rows.astype(jnp.bfloat16), "seq", bit_no).astype(block_rows.dtype)


def double_up(block_rows, bit_list, sender):
    position = lax.axis_index("seq")
    for bit_no in bit_list:
        partner_rows = sender(block_rows, bit_no)
        upper_half = position // 2**bit_no % 2 == 1
        block_rows = jnp.where(
            upper_half,
            jnp.concatenate([partner_rows, block_rows], 0),
            jnp.concatenate([block_rows, partner_rows], 0),
        )
    return block_rows


def halve_down(buffer, bit_list, sender):
    position = lax.axis_index("seq")
    for bit_no in reversed(bit_list):
        half_rows = buffer.shape[0] // 2
        lower_part, upper_part = (buffer[:half_rows], buffer[half_rows:])
        upper_half = position // 2**bit_no % 2 == 1
        kept_half = jnp.where(upper_half, upper_part, lower_part)
        given_half = jnp.where(upper_half, lower_part, upper_part)
        buffer = kept_half + sender(given_half, bit_no)
    return buffer


def head_blocks(heads_here):
    block_width = min(heads_here, 4)
    return [
        (first, min(first + block_width, heads_here)) for first in range(0, heads_here, block_width)
    ]


def forward_level(query_seg, key_seg, value_seg, factor):
    largest_list, total_list, summed_list = ([], [], [])
    for first, last in head_blocks(query_seg.shape[2]):
        scores = (
            jnp.einsum(
                "nihd,njhd->nhij",
                query_seg[:, :, first:last],
                key_seg[:, :, first:last],
                preferred_element_type=jnp.float32,
            )
            * factor
        )
        largest = jnp.max(scores, axis=3)
        powers = jnp.exp(scores - largest[..., None])
        largest_list.append(largest)
        total_list.append(jnp.sum(powers, axis=3))
        summed_list.append(
            jnp.einsum(
                "nhij,njhd->nihd",
                powers.astype(jnp.bfloat16),
                value_seg[:, :, first:last],
                preferred_element_type=jnp.float32,
            )
        )
    return (
        jnp.concatenate(largest_list, 1),
        jnp.concatenate(total_list, 1),
        jnp.concatenate(summed_list, 2),
    )


def level_grads(query_seg, key_seg, value_seg, outgrad_seg, total_seg, dot_seg, factor):
    query_list, key_list, value_list = ([], [], [])
    for first, last in head_blocks(query_seg.shape[2]):
        query_part = query_seg[:, :, first:last]
        key_block = key_seg[:, :, first:last]
        outgrad_part = outgrad_seg[:, :, first:last]
        scores = (
            jnp.einsum("nihd,njhd->nhij", query_part, key_block, preferred_element_type=jnp.float32)
            * factor
        )
        weights = jnp.exp(scores - total_seg[:, first:last, :, None])
        grad_prob = jnp.einsum(
            "nihd,njhd->nhij",
            outgrad_part,
            value_seg[:, :, first:last],
            preferred_element_type=jnp.float32,
        )
        grad_score = (weights * (grad_prob - dot_seg[:, first:last, :, None])).astype(jnp.bfloat16)
        query_list.append(
            jnp.einsum("nhij,njhd->nihd", grad_score, key_block, preferred_element_type=jnp.float32)
            * factor
        )
        key_list.append(
            jnp.einsum(
                "nhij,nihd->njhd", grad_score, query_part, preferred_element_type=jnp.float32
            )
            * factor
        )
        value_list.append(
            jnp.einsum(
                "nhij,nihd->njhd",
                weights.astype(jnp.bfloat16),
                outgrad_part,
                preferred_element_type=jnp.float32,
            )
        )
    query_grad = jnp.concatenate(query_list, 2)
    key_grad = jnp.concatenate(key_list, 2)
    value_grad = jnp.concatenate(value_list, 2)
    return (query_grad, key_grad, value_grad)


def general_body(queries, key_rows, value_rows, grad_out, offsets):
    row_count = queries.shape[0]
    width_here = queries.shape[1]
    heads_here = width_here // HDIM
    factor = HDIM ** (-0.5)
    seq_count = lax.axis_size("seq")
    segment = row_count * seq_count // 2 ** (LEVELS - 1)
    head_first = lax.axis_index("head") * heads_here
    offsets_here = lax.dynamic_slice_in_dim(offsets, head_first, heads_here, 1)
    query_all = queries.reshape(row_count, heads_here, HDIM)
    key_all = key_rows.reshape(row_count, heads_here, HDIM)
    value_all = value_rows.reshape(row_count, heads_here, HDIM)
    outgrad_all = grad_out.reshape(row_count, heads_here, HDIM)
    levels_kept = []
    for level_no in range(LEVELS):
        stride = 2**level_no
        seg_span = segment * stride
        picked = row_count // stride
        level_offsets = offsets_here[level_no]
        query_lev = pick_rows(query_all, level_offsets, stride)
        key_lev = pick_rows(key_all, level_offsets, stride)
        value_lev = pick_rows(value_all, level_offsets, stride)
        if seg_span <= row_count:
            pieces = row_count // seg_span
            bit_list = []
            query_seg = query_lev.reshape(pieces, segment, heads_here, HDIM)
            key_seg = key_lev.reshape(pieces, segment, heads_here, HDIM)
            value_seg = value_lev.reshape(pieces, segment, heads_here, HDIM)
        else:
            group_size = seg_span // row_count
            packed = jnp.concatenate(
                [key_lev.reshape(picked, width_here), value_lev.reshape(picked, width_here)], 1
            )
            if group_size == seq_count:
                bit_list = list(range(group_size.bit_length() - 1))
                gathered = lax.all_gather(packed, "seq", axis=0, tiled=True)
            else:
                bit_list = pair_bits(group_size.bit_length() - 1)
                gathered = double_up(packed, bit_list, send_pairs)
            query_seg = query_lev.reshape(1, picked, heads_here, HDIM)
            key_seg = gathered[:, :width_here].reshape(1, segment, heads_here, HDIM)
            value_seg = gathered[:, width_here:].reshape(1, segment, heads_here, HDIM)
        largest, totals, summed = forward_level(query_seg, key_seg, value_seg, factor)
        level_max = spread_rows(
            jnp.transpose(largest, (0, 2, 1)).reshape(picked, heads_here),
            level_offsets,
            stride,
            -jnp.inf,
        )
        level_total = spread_rows(
            jnp.transpose(totals, (0, 2, 1)).reshape(picked, heads_here), level_offsets, stride, 0.0
        )
        level_sum = spread_rows(
            summed.reshape(picked, heads_here, HDIM), level_offsets, stride, 0.0
        )
        if level_no == 0:
            running_max, running_total, running_sum = (level_max, level_total, level_sum)
        else:
            newest_max = jnp.maximum(running_max, level_max)
            old_scale = jnp.exp(running_max - newest_max)
            new_scale = jnp.exp(level_max - newest_max)
            running_total = running_total * old_scale + level_total * new_scale
            running_sum = running_sum * old_scale[..., None] + level_sum * new_scale[..., None]
            running_max = newest_max
        levels_kept.append(
            (
                stride,
                level_offsets,
                seg_span,
                bit_list,
                query_lev,
                key_lev,
                value_lev,
                query_seg,
                key_seg,
                value_seg,
            )
        )
    attended = (running_sum / running_total[..., None]).astype(jnp.bfloat16)
    log_total = running_max + jnp.log(running_total)
    dot_rows = jnp.sum(outgrad_all.astype(jnp.float32) * attended.astype(jnp.float32), axis=2)
    grad_q_sum = jnp.zeros((row_count, heads_here, HDIM), jnp.float32)
    grad_k_sum = jnp.zeros((row_count, heads_here, HDIM), jnp.float32)
    grad_v_sum = jnp.zeros((row_count, heads_here, HDIM), jnp.float32)
    for (
        stride,
        level_offsets,
        seg_span,
        bit_list,
        query_lev,
        key_lev,
        value_lev,
        query_seg,
        key_seg,
        value_seg,
    ) in levels_kept:
        picked = row_count // stride
        outgrad_lev = pick_rows(outgrad_all, level_offsets, stride)
        total_lev = pick_rows(log_total, level_offsets, stride)
        dot_lev = pick_rows(dot_rows, level_offsets, stride)
        pieces = query_seg.shape[0]
        rows_each = query_seg.shape[1]
        outgrad_seg = outgrad_lev.reshape(pieces, rows_each, heads_here, HDIM)
        total_seg = jnp.transpose(total_lev.reshape(pieces, rows_each, heads_here), (0, 2, 1))
        dot_seg = jnp.transpose(dot_lev.reshape(pieces, rows_each, heads_here), (0, 2, 1))
        if seg_span <= row_count:
            grad_query_lev, key_part, value_part = level_grads(
                query_seg, key_seg, value_seg, outgrad_seg, total_seg, dot_seg, factor
            )
            key_grad = key_part.reshape(picked, heads_here, HDIM)
            value_grad = value_part.reshape(picked, heads_here, HDIM)
        else:
            grad_query_lev, key_part, value_part = level_grads(
                query_seg, key_seg, value_seg, outgrad_seg, total_seg, dot_seg, factor
            )
            packed = jnp.concatenate(
                [key_part.reshape(segment, width_here), value_part.reshape(segment, width_here)], 1
            )
            own_rows = halve_down(packed, bit_list, send_partials)
            key_grad = own_rows[:, :width_here].reshape(picked, heads_here, HDIM)
            value_grad = own_rows[:, width_here:].reshape(picked, heads_here, HDIM)
        grad_q_sum = grad_q_sum + spread_rows(
            grad_query_lev.reshape(picked, heads_here, HDIM), level_offsets, stride, 0.0
        )
        grad_k_sum = grad_k_sum + spread_rows(key_grad, level_offsets, stride, 0.0)
        grad_v_sum = grad_v_sum + spread_rows(value_grad, level_offsets, stride, 0.0)
    return (
        attended.reshape(row_count, width_here),
        grad_q_sum.reshape(row_count, width_here).astype(jnp.bfloat16),
        grad_k_sum.reshape(row_count, width_here).astype(jnp.bfloat16),
        grad_v_sum.reshape(row_count, width_here).astype(jnp.bfloat16),
    )


SEG = 8
LOCAL = 5
NEG = -1e30
NN = (((1,), (0,)), ((), ()))
NT = (((1,), (1,)), ((), ()))


def mm(lhs, rhs, dims=NN):
    return lax.dot_general(lhs, rhs, dims, preferred_element_type=jnp.float32)


def flipped(block):
    return block.astype(jnp.bfloat16).T


def window(head_no):
    first = head_no * HDIM
    return first // 128 * 128, -(-(first + HDIM) // 128) * 128


def zero_extended(rows, head_no):
    low, high = window(head_no)
    first = head_no * HDIM
    parts = []
    if first > low:
        parts.append(jnp.zeros((first - low, rows.shape[1]), rows.dtype))
    parts.append(rows[first : first + HDIM])
    if high > first + HDIM:
        parts.append(jnp.zeros((high - first - HDIM, rows.shape[1]), rows.dtype))
    return parts[0] if len(parts) == 1 else jnp.concatenate(parts, 0)


def kernel(
    seq_count, heads, offs_hbm, q_hbm, k_hbm, v_hbm, g_hbm,
    att_out, dq_out, dk_out, dv_out,
    offs, q_ref, k_ref, v_ref, g_ref, att_ref, dq_ref, dk_ref, dv_ref, fetch,
    buf_kv, buf_qg, stat, e_scr, dp_scr,
    send_kv, recv_kv, send_qg, recv_qg, send_st, recv_st,
):
    me = lax.axis_index("seq")
    fetches = [
        pltpu.make_async_copy(here, there, fetch.at[i])
        for i, (here, there) in enumerate(
            ((offs_hbm, offs), (q_hbm, q_ref), (k_hbm, k_ref), (v_hbm, v_ref), (g_hbm, g_ref))
        )
    ]
    for copy in fetches:
        copy.start()
    f32, bf16 = jnp.float32, jnp.bfloat16
    factor = HDIM ** (-0.5)
    factor2 = factor * math.log2(math.e)
    rows = q_ref.shape[0]
    width = q_ref.shape[1]
    head_first = lax.axis_index("head") * heads

    def peer(dist):
        low = lax.rem(me, 2)
        mid = lax.rem(me // 2, 2)
        top = me // 4
        b0, b1, b2 = dist & 1, dist >> 1 & 1, dist >> 2
        low = 1 - low if b0 else low
        mid = 1 - mid if b1 else mid
        top = 1 - top if b2 else top
        return top * 4 + mid * 2 + low

    barrier = pltpu.get_barrier_semaphore()
    for dist in range(1, seq_count):
        pl.semaphore_signal(
            barrier, inc=1, device_id={"seq": peer(dist)}, device_id_type=pl.DeviceIdType.MESH
        )

    for copy in fetches:
        copy.wait()
    off = [[offs[lev, head_first + h] for h in range(heads)] for lev in range(LEVELS)]
    refs = (q_ref, k_ref, v_ref, g_ref)

    slot_no = lax.broadcasted_iota(jnp.int32, (SEG, rows), 0)
    lane_no = lax.broadcasted_iota(jnp.int32, (SEG, rows), 1)
    picks = []
    for h in range(heads):
        target = jnp.where(
            slot_no < 4,
            slot_no * 32 + off[5][h],
            jnp.where(slot_no < 6, (slot_no - 4) * 64 + off[6][h], off[7][h]),
        )
        target = jnp.where(slot_no == 7, -1, target)
        picks.append(target == lane_no)
    chosen = jnp.concatenate([jnp.where(p, 1.0, 0.0) for p in picks], 0).astype(bf16)
    col_head = lax.broadcasted_iota(jnp.int32, (SEG, width), 1)
    owns = []
    for a in range(4):
        got = mm(chosen, refs[a][...])
        own = jnp.zeros((SEG, width), f32)
        for h in range(heads):
            inside = (col_head >= h * HDIM) & (col_head < (h + 1) * HDIM)
            own = jnp.where(inside, got[h * SEG : (h + 1) * SEG], own)
        owns.append(own)
    q_own, k_own, v_own, g_own = owns
    last_row = lax.broadcasted_iota(jnp.int32, (SEG, width), 0) == SEG - 1
    k_own = jnp.where(last_row, q_own[6:7], k_own)
    v_own = jnp.where(last_row, g_own[6:7], v_own)
    buf_kv[0] = jnp.concatenate([k_own, v_own], 0).astype(bf16)
    buf_qg[0] = jnp.concatenate([q_own, g_own], 0).astype(bf16)

    pl.semaphore_wait(barrier, seq_count - 1)

    def remote(buf, send, recv, dist):
        return pltpu.make_async_remote_copy(
            src_ref=buf.at[0],
            dst_ref=buf.at[dist],
            send_sem=send.at[dist],
            recv_sem=recv.at[dist],
            device_id={"seq": peer(dist)},
            device_id_type=pl.DeviceIdType.MESH,
        )

    first = [remote(buf_kv, send_kv, recv_kv, d) for d in (7, 6, 5, 4, 3, 2, 1)]
    first += [remote(buf_qg, send_qg, recv_qg, d) for d in (3, 2, 1)]
    for copy in first:
        copy.start()

    qt, kt, vt, gt = [flipped(r[...]) for r in refs]

    feat_no = lax.broadcasted_iota(jnp.int32, (32, rows), 0)
    pos = lax.broadcasted_iota(jnp.int32, (32, rows), 1)
    feats = []
    starts = (0, 16, 24, 28, 30)
    place = feat_no - 0
    seg_of = pos // 8
    rest = pos & 0
    for lev in range(1, LOCAL):
        past = feat_no >= starts[lev]
        place = jnp.where(past, feat_no - starts[lev], place)
        seg_of = jnp.where(past, pos // (8 << lev), seg_of)
        rest = jnp.where(past, pos & ((1 << lev) - 1), rest)
    in_seg = (place == seg_of) & (feat_no < 31)
    for h in range(heads):
        wanted = jnp.where(feat_no >= 16, off[1][h], 0)
        for lev in range(2, LOCAL):
            wanted = jnp.where(feat_no >= starts[lev], off[lev][h], wanted)
        feats.append(jnp.where(in_seg & (rest == wanted), 1.0, 0.0))
    feat_rows = [
        jnp.concatenate(feats[4 * b : 4 * b + 4], 0).T.astype(bf16) for b in range(heads // 4)
    ]
    tops, sums, dots = [], [], []
    lane8 = lax.broadcasted_iota(jnp.int32, (SEG, 128), 1)
    row8 = lax.broadcasted_iota(jnp.int32, (SEG, 128), 0)
    note = jnp.where((row8 == SEG - 1) & (lane8 >= heads) & (lane8 < 2 * heads), 1.0, 0.0)
    for h in range(heads):
        low, high = window(h)
        before = 32 * (h % 4)
        parts = [jnp.zeros((before, rows), bf16)] if before else []
        parts.append(feats[h].astype(bf16))
        if before < 96:
            parts.append(jnp.zeros((96 - before, rows), bf16))
        count = mm(feat_rows[h // 4], jnp.concatenate(parts, 0))
        score = mm(k_ref[:, low:high], zero_extended(qt, h)) * factor2
        score = jnp.where(count > 0, score, NEG)
        top = jnp.max(score, axis=0, keepdims=True)
        near = count * jnp.exp2(score - top)
        dp = mm(v_ref[:, low:high], zero_extended(gt, h))
        e_scr[h] = near
        dp_scr[h] = dp
        total = jnp.sum(near, axis=0, keepdims=True)
        dot = jnp.sum(near * dp, axis=0, keepdims=True)
        tops.append(top)
        sums.append(total)
        dots.append(dot)
        for kind, row in enumerate((top, total, dot)):
            column = jnp.sum(jnp.where(picks[h], row, 0.0), axis=1, keepdims=True)
            here = (lane8 == kind * heads + h) & (row8 < SEG - 1)
            note = jnp.where(here, column, note)
    stat[0] = note
    second = [remote(stat, send_st, recv_st, d) for d in (7, 6, 5, 4, 3, 2, 1)]
    for copy in second:
        copy.start()

    far_n = SEG * seq_count
    query_n = 5 * SEG
    key_no = lax.broadcasted_iota(jnp.int32, (far_n, 128), 0)
    key_slot = key_no & 7
    key_dist = key_no >> 3
    lane_pos = lax.broadcasted_iota(jnp.int32, (far_n, 128), 1)
    key_span = jnp.where(key_slot < 4, 31, jnp.where(key_slot < 6, 63, 127))
    key_reach = jnp.where(key_slot < 4, 1, jnp.where(key_slot < 6, 2, 3))
    lane_rest = lane_pos & key_span
    lane_ok = (key_dist >> key_reach) == 0

    def query_marks(shape):
        number = lax.broadcasted_iota(jnp.int32, shape, 1)
        dist = jnp.where(number < 32, number >> 3, number - 32)
        slot = jnp.where(number < 32, number & 7, 6)
        return number, dist, slot

    _, dist_b, slot_b = query_marks((far_n, query_n))
    pair_ok = ((dist_b ^ key_dist[:, :query_n]) >> key_reach[:, :query_n]) == 0
    number_c, dist_c, slot_c = query_marks((rows, query_n))
    reach_c = jnp.where(slot_c < 4, 1, jnp.where(slot_c < 6, 2, 3))
    span_c = jnp.where(slot_c < 4, 31, jnp.where(slot_c < 6, 63, 127))
    own_pos = lax.broadcasted_iota(jnp.int32, (rows, query_n), 0)
    rest_c = own_pos & span_c
    ok_c = ((dist_c >> reach_c) == 0) & (slot_c != 7) & ((number_c < 32) | (dist_c >= 4))

    for copy in first:
        copy.wait()
    kv = buf_kv[...].astype(f32)
    qg = buf_qg[...].astype(f32)
    k_far32 = kv[:, 0:SEG].reshape(far_n, width)
    v_far32 = kv[:, SEG:].reshape(far_n, width)
    q_far32 = jnp.concatenate(
        [qg[:, 0:SEG].reshape(4 * SEG, width)] + [kv[d, SEG - 1 : SEG] for d in range(8)], 0
    )
    g_far32 = jnp.concatenate(
        [qg[:, SEG:].reshape(4 * SEG, width)] + [kv[d, 2 * SEG - 1 : 2 * SEG] for d in range(8)], 0
    )
    k_far, v_far = k_far32.astype(bf16), v_far32.astype(bf16)
    k_ft, v_ft, q_ft, g_ft = [
        x.T.astype(bf16) for x in (k_far32, v_far32, q_far32, g_far32)
    ]
    for copy in second:
        copy.wait()
    st = stat[...]
    notes = jnp.concatenate(
        [st[0:4].reshape(4 * SEG, 128)] + [st[d, 6:7] for d in range(8)], 0
    ).T

    for h in range(heads):
        low, high = window(h)
        cut = slice(h * HDIM, (h + 1) * HDIM)
        qz, gz = zero_extended(qt, h), zero_extended(gt, h)
        qfz, gfz = zero_extended(q_ft, h), zero_extended(g_ft, h)
        wanted = jnp.where(key_slot < 4, off[5][h], jnp.where(key_slot < 6, off[6][h], off[7][h]))
        wanted = jnp.where(key_slot == 7, -1, wanted)
        far = mm(k_far[:, low:high], qz) * factor2
        far = jnp.where(lane_ok & (lane_rest == wanted), far, NEG)
        dp_far = mm(v_far[:, low:high], gz)
        top = jnp.maximum(tops[h], jnp.max(far, axis=0, keepdims=True))
        e_far = jnp.exp2(far - top)
        shrink = jnp.exp2(tops[h] - top)
        total = sums[h] * shrink + jnp.sum(e_far, axis=0, keepdims=True)
        inv = 1.0 / total
        delta = (dots[h] * shrink + jnp.sum(e_far * dp_far, axis=0, keepdims=True)) * inv
        near = e_scr[h] * (shrink * inv)
        e_far = e_far * inv
        near_low, far_low = near.astype(bf16), e_far.astype(bf16)
        ds = (near * (dp_scr[h] - delta)).astype(bf16)
        ds_far = (e_far * (dp_far - delta)).astype(bf16)
        att_ref[cut, :] = mm(vt[cut], near_low) + mm(v_ft[cut], far_low)
        dq_ref[cut, :] = (mm(kt[cut], ds) + mm(k_ft[cut], ds_far)) * factor
        spot = jnp.where(
            slot_b < 4,
            slot_b * 32 + off[5][h],
            jnp.where(slot_b < 6, (slot_b - 4) * 64 + off[6][h], off[7][h]),
        )
        meets = pair_ok & ((spot & key_span[:, :query_n]) == wanted[:, :query_n])
        other = jnp.where(meets, mm(k_far[:, low:high], qfz) * factor2, NEG)
        dp_other = mm(v_far[:, low:high], gfz)
        near_top = notes[h : h + 1]
        top = jnp.maximum(near_top, jnp.max(other, axis=0, keepdims=True))
        e_other = jnp.exp2(other - top)
        shrink = jnp.exp2(near_top - top)
        total = notes[heads + h : heads + h + 1] * shrink + jnp.sum(
            e_other, axis=0, keepdims=True
        )
        delta = (
            notes[2 * heads + h : 2 * heads + h + 1] * shrink
            + jnp.sum(e_other * dp_other, axis=0, keepdims=True)
        ) / total
        lse = top + jnp.log2(total)
        wanted_c = jnp.where(slot_c < 4, off[5][h], jnp.where(slot_c < 6, off[6][h], off[7][h]))
        score = mm(k_ref[:, low:high], qfz) * factor2
        prob = jnp.exp2(jnp.where(ok_c & (rest_c == wanted_c), score - lse, NEG))
        ds_own = (prob * (mm(v_ref[:, low:high], gfz) - delta)).astype(bf16)
        dk_ref[cut, :] = (mm(qt[cut], ds, NT) + mm(q_ft[cut], ds_own, NT)) * factor
        dv_ref[cut, :] = mm(gt[cut], near_low, NT) + mm(g_ft[cut], prob.astype(bf16), NT)
    att_out[...] = flipped(att_ref[...])
    dq_out[...] = flipped(dq_ref[...])
    dk_out[...] = flipped(dk_ref[...])
    dv_out[...] = flipped(dv_ref[...])


def write_out(*refs):
    ends = refs[8]
    copies = [pltpu.make_async_copy(refs[i], refs[4 + i], ends.at[i]) for i in range(4)]
    for copy in copies:
        copy.start()
    for copy in copies:
        copy.wait()


def small_body(queries, key_rows, value_rows, grad_out, offsets):
    rows, width = queries.shape
    heads = width // HDIM
    seq_count = lax.axis_size("seq")
    hbm = pl.BlockSpec(memory_space=pltpu.HBM)
    vmem = pl.BlockSpec(memory_space=pltpu.VMEM)
    dma = pltpu.SemaphoreType.DMA
    outs = pl.pallas_call(
        functools.partial(kernel, seq_count, heads),
        out_shape=[jax.ShapeDtypeStruct((rows, width), jnp.bfloat16)] * 4,
        in_specs=[hbm] * 5,
        out_specs=[vmem] * 4,
        scratch_shapes=[
            pltpu.SMEM(offsets.shape, jnp.int32),
            *[pltpu.VMEM((rows, width), jnp.bfloat16)] * 4,
            *[pltpu.VMEM((width, rows), jnp.float32)] * 4,
            dma((5,)),
            pltpu.VMEM((8, 16, width), jnp.bfloat16),
            pltpu.VMEM((4, 16, width), jnp.bfloat16),
            pltpu.VMEM((8, SEG, 128), jnp.float32),
            pltpu.VMEM((heads, rows, rows), jnp.float32),
            pltpu.VMEM((heads, rows, rows), jnp.float32),
            dma((8,)), dma((8,)), dma((4,)), dma((4,)), dma((8,)), dma((8,)),
        ],
        compiler_params=pltpu.CompilerParams(
            collective_id=0, has_side_effects=True, vmem_limit_bytes=62 * 2**20
        ),
    )(offsets, queries, key_rows, value_rows, grad_out)
    return pl.pallas_call(
        write_out,
        out_shape=[jax.ShapeDtypeStruct((rows, width), jnp.bfloat16)] * 4,
        in_specs=[vmem] * 4,
        out_specs=[hbm] * 4,
        scratch_shapes=[dma((4,))],
    )(*outs)


def body(queries, key_rows, value_rows, grad_out, offsets):
    rows, width = queries.shape
    seq_count = lax.axis_size("seq")
    if seq_count == 8 and rows == 128 and width == 8 * HDIM:
        return small_body(queries, key_rows, value_rows, grad_out, offsets)
    return general_body(queries, key_rows, value_rows, grad_out, offsets)


def solution(mesh):
    placed = (
        P(("groups", "seq"), "head"),
        P(("groups", "seq"), "head"),
        P(("groups", "seq"), "head"),
        P(("groups", "seq"), "head"),
        P(),
    )
    return jax.shard_map(
        body,
        mesh=mesh,
        in_specs=placed,
        out_specs=(
            P(("groups", "seq"), "head"),
            P(("groups", "seq"), "head"),
            P(("groups", "seq"), "head"),
            P(("groups", "seq"), "head"),
        ),
        check_vma=False,
    )
```

```python
import functools
import math

import jax
import jax.numpy as jnp
from jax import lax
from jax.experimental import pallas as pl
from jax.experimental.pallas import tpu as pltpu
from jax.sharding import PartitionSpec as P

HDIM = 48
LEVELS = 8


def swapped(shard, axis, bit):
    return lax.ppermute(shard, axis, [(i, i ^ 1 << bit) for i in range(lax.axis_size(axis))])


def pick_rows(values, level_offsets, stride):
    if stride == 1:
        return values
    length, head_count = (values.shape[0], values.shape[1])
    trailing = values.shape[2:]
    grouped = values.reshape((length // stride, stride, head_count) + trailing)
    marks = jnp.arange(stride, dtype=jnp.int32)[:, None] == level_offsets[None, :]
    marks = marks.reshape((1, stride, head_count) + (1,) * len(trailing))
    kept = jnp.where(marks, grouped, jnp.zeros((), values.dtype))
    return jnp.sum(kept, axis=1, dtype=values.dtype)


def spread_rows(values, level_offsets, stride, fill):
    count, head_count = (values.shape[0], values.shape[1])
    trailing = values.shape[2:]
    marks = jnp.arange(stride, dtype=jnp.int32)[:, None] == level_offsets[None, :]
    marks = marks.reshape((1, stride, head_count) + (1,) * len(trailing))
    placed = jnp.where(marks, values[:, None], jnp.asarray(fill, values.dtype))
    return placed.reshape((count * stride, head_count) + trailing)


def pair_bits(count):
    return list(range(count))


def send_pairs(block_rows, bit_no):
    return swapped(block_rows, "seq", bit_no)


def send_partials(block_rows, bit_no):
    return swapped(block_rows.astype(jnp.bfloat16), "seq", bit_no).astype(block_rows.dtype)


def double_up(block_rows, bit_list, sender):
    position = lax.axis_index("seq")
    for bit_no in bit_list:
        partner_rows = sender(block_rows, bit_no)
        upper_half = position // 2**bit_no % 2 == 1
        block_rows = jnp.where(
            upper_half,
            jnp.concatenate([partner_rows, block_rows], 0),
            jnp.concatenate([block_rows, partner_rows], 0),
        )
    return block_rows


def halve_down(buffer, bit_list, sender):
    position = lax.axis_index("seq")
    for bit_no in reversed(bit_list):
        half_rows = buffer.shape[0] // 2
        lower_part, upper_part = (buffer[:half_rows], buffer[half_rows:])
        upper_half = position // 2**bit_no % 2 == 1
        kept_half = jnp.where(upper_half, upper_part, lower_part)
        given_half = jnp.where(upper_half, lower_part, upper_part)
        buffer = kept_half + sender(given_half, bit_no)
    return buffer


def head_blocks(heads_here):
    block_width = min(heads_here, 4)
    return [
        (first, min(first + block_width, heads_here)) for first in range(0, heads_here, block_width)
    ]


def forward_level(query_seg, key_seg, value_seg, factor):
    largest_list, total_list, summed_list = ([], [], [])
    for first, last in head_blocks(query_seg.shape[2]):
        scores = (
            jnp.einsum(
                "nihd,njhd->nhij",
                query_seg[:, :, first:last],
                key_seg[:, :, first:last],
                preferred_element_type=jnp.float32,
            )
            * factor
        )
        largest = jnp.max(scores, axis=3)
        powers = jnp.exp(scores - largest[..., None])
        largest_list.append(largest)
        total_list.append(jnp.sum(powers, axis=3))
        summed_list.append(
            jnp.einsum(
                "nhij,njhd->nihd",
                powers.astype(jnp.bfloat16),
                value_seg[:, :, first:last],
                preferred_element_type=jnp.float32,
            )
        )
    return (
        jnp.concatenate(largest_list, 1),
        jnp.concatenate(total_list, 1),
        jnp.concatenate(summed_list, 2),
    )


def level_grads(query_seg, key_seg, value_seg, outgrad_seg, total_seg, dot_seg, factor):
    query_list, key_list, value_list = ([], [], [])
    for first, last in head_blocks(query_seg.shape[2]):
        query_part = query_seg[:, :, first:last]
        key_block = key_seg[:, :, first:last]
        outgrad_part = outgrad_seg[:, :, first:last]
        scores = (
            jnp.einsum("nihd,njhd->nhij", query_part, key_block, preferred_element_type=jnp.float32)
            * factor
        )
        weights = jnp.exp(scores - total_seg[:, first:last, :, None])
        grad_prob = jnp.einsum(
            "nihd,njhd->nhij",
            outgrad_part,
            value_seg[:, :, first:last],
            preferred_element_type=jnp.float32,
        )
        grad_score = (weights * (grad_prob - dot_seg[:, first:last, :, None])).astype(jnp.bfloat16)
        query_list.append(
            jnp.einsum("nhij,njhd->nihd", grad_score, key_block, preferred_element_type=jnp.float32)
            * factor
        )
        key_list.append(
            jnp.einsum(
                "nhij,nihd->njhd", grad_score, query_part, preferred_element_type=jnp.float32
            )
            * factor
        )
        value_list.append(
            jnp.einsum(
                "nhij,nihd->njhd",
                weights.astype(jnp.bfloat16),
                outgrad_part,
                preferred_element_type=jnp.float32,
            )
        )
    query_grad = jnp.concatenate(query_list, 2)
    key_grad = jnp.concatenate(key_list, 2)
    value_grad = jnp.concatenate(value_list, 2)
    return (query_grad, key_grad, value_grad)


def general_body(queries, key_rows, value_rows, grad_out, offsets):
    row_count = queries.shape[0]
    width_here = queries.shape[1]
    heads_here = width_here // HDIM
    factor = HDIM ** (-0.5)
    seq_count = lax.axis_size("seq")
    segment = row_count * seq_count // 2 ** (LEVELS - 1)
    head_first = lax.axis_index("head") * heads_here
    offsets_here = lax.dynamic_slice_in_dim(offsets, head_first, heads_here, 1)
    query_all = queries.reshape(row_count, heads_here, HDIM)
    key_all = key_rows.reshape(row_count, heads_here, HDIM)
    value_all = value_rows.reshape(row_count, heads_here, HDIM)
    outgrad_all = grad_out.reshape(row_count, heads_here, HDIM)
    levels_kept = []
    for level_no in range(LEVELS):
        stride = 2**level_no
        seg_span = segment * stride
        picked = row_count // stride
        level_offsets = offsets_here[level_no]
        query_lev = pick_rows(query_all, level_offsets, stride)
        key_lev = pick_rows(key_all, level_offsets, stride)
        value_lev = pick_rows(value_all, level_offsets, stride)
        if seg_span <= row_count:
            pieces = row_count // seg_span
            bit_list = []
            query_seg = query_lev.reshape(pieces, segment, heads_here, HDIM)
            key_seg = key_lev.reshape(pieces, segment, heads_here, HDIM)
            value_seg = value_lev.reshape(pieces, segment, heads_here, HDIM)
        else:
            group_size = seg_span // row_count
            packed = jnp.concatenate(
                [key_lev.reshape(picked, width_here), value_lev.reshape(picked, width_here)], 1
            )
            if group_size == seq_count:
                bit_list = list(range(group_size.bit_length() - 1))
                gathered = lax.all_gather(packed, "seq", axis=0, tiled=True)
            else:
                bit_list = pair_bits(group_size.bit_length() - 1)
                gathered = double_up(packed, bit_list, send_pairs)
            query_seg = query_lev.reshape(1, picked, heads_here, HDIM)
            key_seg = gathered[:, :width_here].reshape(1, segment, heads_here, HDIM)
            value_seg = gathered[:, width_here:].reshape(1, segment, heads_here, HDIM)
        largest, totals, summed = forward_level(query_seg, key_seg, value_seg, factor)
        level_max = spread_rows(
            jnp.transpose(largest, (0, 2, 1)).reshape(picked, heads_here),
            level_offsets,
            stride,
            -jnp.inf,
        )
        level_total = spread_rows(
            jnp.transpose(totals, (0, 2, 1)).reshape(picked, heads_here), level_offsets, stride, 0.0
        )
        level_sum = spread_rows(
            summed.reshape(picked, heads_here, HDIM), level_offsets, stride, 0.0
        )
        if level_no == 0:
            running_max, running_total, running_sum = (level_max, level_total, level_sum)
        else:
            newest_max = jnp.maximum(running_max, level_max)
            old_scale = jnp.exp(running_max - newest_max)
            new_scale = jnp.exp(level_max - newest_max)
            running_total = running_total * old_scale + level_total * new_scale
            running_sum = running_sum * old_scale[..., None] + level_sum * new_scale[..., None]
            running_max = newest_max
        levels_kept.append(
            (
                stride,
                level_offsets,
                seg_span,
                bit_list,
                query_lev,
                key_lev,
                value_lev,
                query_seg,
                key_seg,
                value_seg,
            )
        )
    attended = (running_sum / running_total[..., None]).astype(jnp.bfloat16)
    log_total = running_max + jnp.log(running_total)
    dot_rows = jnp.sum(outgrad_all.astype(jnp.float32) * attended.astype(jnp.float32), axis=2)
    grad_q_sum = jnp.zeros((row_count, heads_here, HDIM), jnp.float32)
    grad_k_sum = jnp.zeros((row_count, heads_here, HDIM), jnp.float32)
    grad_v_sum = jnp.zeros((row_count, heads_here, HDIM), jnp.float32)
    for (
        stride,
        level_offsets,
        seg_span,
        bit_list,
        query_lev,
        key_lev,
        value_lev,
        query_seg,
        key_seg,
        value_seg,
    ) in levels_kept:
        picked = row_count // stride
        outgrad_lev = pick_rows(outgrad_all, level_offsets, stride)
        total_lev = pick_rows(log_total, level_offsets, stride)
        dot_lev = pick_rows(dot_rows, level_offsets, stride)
        pieces = query_seg.shape[0]
        rows_each = query_seg.shape[1]
        outgrad_seg = outgrad_lev.reshape(pieces, rows_each, heads_here, HDIM)
        total_seg = jnp.transpose(total_lev.reshape(pieces, rows_each, heads_here), (0, 2, 1))
        dot_seg = jnp.transpose(dot_lev.reshape(pieces, rows_each, heads_here), (0, 2, 1))
        if seg_span <= row_count:
            grad_query_lev, key_part, value_part = level_grads(
                query_seg, key_seg, value_seg, outgrad_seg, total_seg, dot_seg, factor
            )
            key_grad = key_part.reshape(picked, heads_here, HDIM)
            value_grad = value_part.reshape(picked, heads_here, HDIM)
        else:
            grad_query_lev, key_part, value_part = level_grads(
                query_seg, key_seg, value_seg, outgrad_seg, total_seg, dot_seg, factor
            )
            packed = jnp.concatenate(
                [key_part.reshape(segment, width_here), value_part.reshape(segment, width_here)], 1
            )
            own_rows = halve_down(packed, bit_list, send_partials)
            key_grad = own_rows[:, :width_here].reshape(picked, heads_here, HDIM)
            value_grad = own_rows[:, width_here:].reshape(picked, heads_here, HDIM)
        grad_q_sum = grad_q_sum + spread_rows(
            grad_query_lev.reshape(picked, heads_here, HDIM), level_offsets, stride, 0.0
        )
        grad_k_sum = grad_k_sum + spread_rows(key_grad, level_offsets, stride, 0.0)
        grad_v_sum = grad_v_sum + spread_rows(value_grad, level_offsets, stride, 0.0)
    return (
        attended.reshape(row_count, width_here),
        grad_q_sum.reshape(row_count, width_here).astype(jnp.bfloat16),
        grad_k_sum.reshape(row_count, width_here).astype(jnp.bfloat16),
        grad_v_sum.reshape(row_count, width_here).astype(jnp.bfloat16),
    )


SEG = 8
LOCAL = 5
NEG = -1e30
NN = (((1,), (0,)), ((), ()))
NT = (((1,), (1,)), ((), ()))


def mm(lhs, rhs, dims=NN):
    return lax.dot_general(lhs, rhs, dims, preferred_element_type=jnp.float32)


def flipped(block):
    return block.astype(jnp.bfloat16).T


def window(head_no):
    first = head_no * HDIM
    return first // 128 * 128, -(-(first + HDIM) // 128) * 128


def zero_extended(rows, head_no):
    low, high = window(head_no)
    first = head_no * HDIM
    parts = []
    if first > low:
        parts.append(jnp.zeros((first - low, rows.shape[1]), rows.dtype))
    parts.append(rows[first : first + HDIM])
    if high > first + HDIM:
        parts.append(jnp.zeros((high - first - HDIM, rows.shape[1]), rows.dtype))
    return parts[0] if len(parts) == 1 else jnp.concatenate(parts, 0)


def kernel(
    seq_count, heads, offs_hbm, q_hbm, k_hbm, v_hbm, g_hbm,
    att_out, dq_out, dk_out, dv_out,
    offs, q_ref, k_ref, v_ref, g_ref, att_ref, dq_ref, dk_ref, dv_ref, fetch,
    buf_kv, buf_qg, stat, e_scr, dp_scr, far_bias, other_bias, own_bias,
    send_kv, recv_kv, send_qg, recv_qg, send_st, recv_st,
):
    me = lax.axis_index("seq")
    fetches = [
        pltpu.make_async_copy(here, there, fetch.at[i])
        for i, (here, there) in enumerate(
            ((offs_hbm, offs), (q_hbm, q_ref), (k_hbm, k_ref), (v_hbm, v_ref), (g_hbm, g_ref))
        )
    ]
    for copy in fetches:
        copy.start()
    f32, bf16 = jnp.float32, jnp.bfloat16
    factor = HDIM ** (-0.5)
    factor2 = factor * math.log2(math.e)
    rows = q_ref.shape[0]
    width = q_ref.shape[1]
    head_first = lax.axis_index("head") * heads

    def peer(dist):
        low = lax.rem(me, 2)
        mid = lax.rem(me // 2, 2)
        top = me // 4
        b0, b1, b2 = dist & 1, dist >> 1 & 1, dist >> 2
        low = 1 - low if b0 else low
        mid = 1 - mid if b1 else mid
        top = 1 - top if b2 else top
        return top * 4 + mid * 2 + low

    barrier = pltpu.get_barrier_semaphore()
    for dist in range(1, seq_count):
        pl.semaphore_signal(
            barrier, inc=1, device_id={"seq": peer(dist)}, device_id_type=pl.DeviceIdType.MESH
        )

    for copy in fetches:
        copy.wait()
    off = [[offs[lev, head_first + h] for h in range(heads)] for lev in range(LEVELS)]
    refs = (q_ref, k_ref, v_ref, g_ref)

    slot_no = lax.broadcasted_iota(jnp.int32, (SEG, rows), 0)
    lane_no = lax.broadcasted_iota(jnp.int32, (SEG, rows), 1)
    picks = []
    for h in range(heads):
        target = jnp.where(
            slot_no < 4,
            slot_no * 32 + off[5][h],
            jnp.where(slot_no < 6, (slot_no - 4) * 64 + off[6][h], off[7][h]),
        )
        target = jnp.where(slot_no == 7, -1, target)
        picks.append(target == lane_no)
    chosen = jnp.concatenate([jnp.where(p, 1.0, 0.0) for p in picks], 0).astype(bf16)
    col_head = lax.broadcasted_iota(jnp.int32, (SEG, width), 1)
    owns = []
    for a in range(4):
        got = mm(chosen, refs[a][...])
        own = jnp.zeros((SEG, width), f32)
        for h in range(heads):
            inside = (col_head >= h * HDIM) & (col_head < (h + 1) * HDIM)
            own = jnp.where(inside, got[h * SEG : (h + 1) * SEG], own)
        owns.append(own)
    q_own, k_own, v_own, g_own = owns
    last_row = lax.broadcasted_iota(jnp.int32, (SEG, width), 0) == SEG - 1
    k_own = jnp.where(last_row, q_own[6:7], k_own)
    v_own = jnp.where(last_row, g_own[6:7], v_own)
    buf_kv[0] = jnp.concatenate([k_own, v_own], 0).astype(bf16)
    buf_qg[0] = jnp.concatenate([q_own, g_own], 0).astype(bf16)

    pl.semaphore_wait(barrier, seq_count - 1)

    def remote(buf, send, recv, dist):
        return pltpu.make_async_remote_copy(
            src_ref=buf.at[0],
            dst_ref=buf.at[dist],
            send_sem=send.at[dist],
            recv_sem=recv.at[dist],
            device_id={"seq": peer(dist)},
            device_id_type=pl.DeviceIdType.MESH,
        )

    first = [remote(buf_kv, send_kv, recv_kv, d) for d in (7, 6, 5, 4, 3, 2, 1)]
    first += [remote(buf_qg, send_qg, recv_qg, d) for d in (3, 2, 1)]
    for copy in first:
        copy.start()

    qt, kt, vt, gt = [flipped(r[...]) for r in refs]

    feat_no = lax.broadcasted_iota(jnp.int32, (32, rows), 0)
    pos = lax.broadcasted_iota(jnp.int32, (32, rows), 1)
    feats = []
    starts = (0, 16, 24, 28, 30)
    place = feat_no - 0
    seg_of = pos // 8
    rest = pos & 0
    for lev in range(1, LOCAL):
        past = feat_no >= starts[lev]
        place = jnp.where(past, feat_no - starts[lev], place)
        seg_of = jnp.where(past, pos // (8 << lev), seg_of)
        rest = jnp.where(past, pos & ((1 << lev) - 1), rest)
    in_seg = (place == seg_of) & (feat_no < 31)
    for h in range(heads):
        wanted = jnp.where(feat_no >= 16, off[1][h], 0)
        for lev in range(2, LOCAL):
            wanted = jnp.where(feat_no >= starts[lev], off[lev][h], wanted)
        feats.append(jnp.where(in_seg & (rest == wanted), 1.0, 0.0))
    feat_rows = [
        jnp.concatenate(feats[4 * b : 4 * b + 4], 0).T.astype(bf16) for b in range(heads // 4)
    ]
    tops, sums, dots = [], [], []
    lane8 = lax.broadcasted_iota(jnp.int32, (SEG, 128), 1)
    row8 = lax.broadcasted_iota(jnp.int32, (SEG, 128), 0)
    note = jnp.where((row8 == SEG - 1) & (lane8 >= heads) & (lane8 < 2 * heads), 1.0, 0.0)
    for h in range(heads):
        low, high = window(h)
        before = 32 * (h % 4)
        parts = [jnp.zeros((before, rows), bf16)] if before else []
        parts.append(feats[h].astype(bf16))
        if before < 96:
            parts.append(jnp.zeros((96 - before, rows), bf16))
        count = mm(feat_rows[h // 4], jnp.concatenate(parts, 0))
        score = mm(k_ref[:, low:high], zero_extended(qt, h)) * factor2
        score = jnp.where(count > 0, score, NEG)
        top = jnp.max(score, axis=0, keepdims=True)
        near = count * jnp.exp2(score - top)
        dp = mm(v_ref[:, low:high], zero_extended(gt, h))
        e_scr[h] = near
        dp_scr[h] = dp
        cut = slice(h * HDIM, (h + 1) * HDIM)
        att_ref[cut, :] = mm(vt[cut], near.astype(bf16))
        total = jnp.sum(near, axis=0, keepdims=True)
        dot = jnp.sum(near * dp, axis=0, keepdims=True)
        tops.append(top)
        sums.append(total)
        dots.append(dot)
        for kind, row in enumerate((top, total, dot)):
            column = jnp.sum(jnp.where(picks[h], row, 0.0), axis=1, keepdims=True)
            here = (lane8 == kind * heads + h) & (row8 < SEG - 1)
            note = jnp.where(here, column, note)
    stat[0] = note
    second = [remote(stat, send_st, recv_st, d) for d in (7, 6, 5, 4, 3, 2, 1)]
    for copy in second:
        copy.start()

    far_n = SEG * seq_count
    query_n = 5 * SEG
    key_no = lax.broadcasted_iota(jnp.int32, (far_n, 128), 0)
    key_slot = key_no & 7
    key_dist = key_no >> 3
    lane_pos = lax.broadcasted_iota(jnp.int32, (far_n, 128), 1)
    key_span = jnp.where(key_slot < 4, 31, jnp.where(key_slot < 6, 63, 127))
    key_reach = jnp.where(key_slot < 4, 1, jnp.where(key_slot < 6, 2, 3))
    lane_rest = lane_pos & key_span
    lane_ok = (key_dist >> key_reach) == 0

    def query_marks(shape):
        number = lax.broadcasted_iota(jnp.int32, shape, 1)
        dist = jnp.where(number < 32, number >> 3, number - 32)
        slot = jnp.where(number < 32, number & 7, 6)
        return number, dist, slot

    _, dist_b, slot_b = query_marks((far_n, query_n))
    pair_ok = ((dist_b ^ key_dist[:, :query_n]) >> key_reach[:, :query_n]) == 0
    number_c, dist_c, slot_c = query_marks((rows, query_n))
    reach_c = jnp.where(slot_c < 4, 1, jnp.where(slot_c < 6, 2, 3))
    span_c = jnp.where(slot_c < 4, 31, jnp.where(slot_c < 6, 63, 127))
    own_pos = lax.broadcasted_iota(jnp.int32, (rows, query_n), 0)
    rest_c = own_pos & span_c
    ok_c = ((dist_c >> reach_c) == 0) & (slot_c != 7) & ((number_c < 32) | (dist_c >= 4))

    for h in range(heads):
        wanted = jnp.where(key_slot < 4, off[5][h], jnp.where(key_slot < 6, off[6][h], off[7][h]))
        wanted = jnp.where(key_slot == 7, -1, wanted)
        far_bias[h] = jnp.where(lane_ok & (lane_rest == wanted), 0.0, NEG)
        spot = jnp.where(
            slot_b < 4,
            slot_b * 32 + off[5][h],
            jnp.where(slot_b < 6, (slot_b - 4) * 64 + off[6][h], off[7][h]),
        )
        meets = pair_ok & ((spot & key_span[:, :query_n]) == wanted[:, :query_n])
        other_bias[h] = jnp.where(meets, 0.0, NEG)
        wanted_c = jnp.where(slot_c < 4, off[5][h], jnp.where(slot_c < 6, off[6][h], off[7][h]))
        own_bias[h] = jnp.where(ok_c & (rest_c == wanted_c), 0.0, NEG)

    for copy in first:
        copy.wait()
    kv = buf_kv[...].astype(f32)
    qg = buf_qg[...].astype(f32)
    k_far32 = kv[:, 0:SEG].reshape(far_n, width)
    v_far32 = kv[:, SEG:].reshape(far_n, width)
    q_far32 = jnp.concatenate(
        [qg[:, 0:SEG].reshape(4 * SEG, width)] + [kv[d, SEG - 1 : SEG] for d in range(8)], 0
    )
    g_far32 = jnp.concatenate(
        [qg[:, SEG:].reshape(4 * SEG, width)] + [kv[d, 2 * SEG - 1 : 2 * SEG] for d in range(8)], 0
    )
    k_far, v_far = k_far32.astype(bf16), v_far32.astype(bf16)
    k_ft, v_ft, q_ft, g_ft = [
        x.T.astype(bf16) for x in (k_far32, v_far32, q_far32, g_far32)
    ]
    cuts = [slice(h * HDIM, (h + 1) * HDIM) for h in range(heads)]
    far_s, far_dp, oth_s, oth_dp, own_s, own_dp = [], [], [], [], [], []
    for h in range(heads):
        low, high = window(h)
        qz, gz = zero_extended(qt, h), zero_extended(gt, h)
        qfz, gfz = zero_extended(q_ft, h), zero_extended(g_ft, h)
        far_s.append(mm(k_far[:, low:high], qz) * factor2 + far_bias[h])
        far_dp.append(mm(v_far[:, low:high], gz))
        oth_s.append(mm(k_far[:, low:high], qfz) * factor2 + other_bias[h])
        oth_dp.append(mm(v_far[:, low:high], gfz))
        own_s.append(mm(k_ref[:, low:high], qfz) * factor2 + own_bias[h])
        own_dp.append(mm(v_ref[:, low:high], gfz))
    near_low, near_ds, far_low, far_ds = [], [], [], []
    for h in range(heads):
        top = jnp.maximum(tops[h], jnp.max(far_s[h], axis=0, keepdims=True))
        e_far = jnp.exp2(far_s[h] - top)
        shrink = jnp.exp2(tops[h] - top)
        total = sums[h] * shrink + jnp.sum(e_far, axis=0, keepdims=True)
        inv = 1.0 / total
        delta = (dots[h] * shrink + jnp.sum(e_far * far_dp[h], axis=0, keepdims=True)) * inv
        scale = shrink * inv
        near = e_scr[h] * scale
        e_far = e_far * inv
        near_low.append(near.astype(bf16))
        far_low.append(e_far.astype(bf16))
        near_ds.append((near * (dp_scr[h] - delta)).astype(bf16))
        far_ds.append((e_far * (far_dp[h] - delta)).astype(bf16))
        att_ref[cuts[h], :] = att_ref[cuts[h], :] * scale
    for h, cut in enumerate(cuts):
        att_ref[cut, :] += mm(v_ft[cut], far_low[h])
        dq_ref[cut, :] = (mm(kt[cut], near_ds[h]) + mm(k_ft[cut], far_ds[h])) * factor
        dk_ref[cut, :] = mm(qt[cut], near_ds[h], NT)
        dv_ref[cut, :] = mm(gt[cut], near_low[h], NT)
    for copy in second:
        copy.wait()
    st = stat[...]
    notes = jnp.concatenate(
        [st[0:4].reshape(4 * SEG, 128)] + [st[d, 6:7] for d in range(8)], 0
    ).T
    own_low, own_ds = [], []
    for h in range(heads):
        near_top = notes[h : h + 1]
        top = jnp.maximum(near_top, jnp.max(oth_s[h], axis=0, keepdims=True))
        e_other = jnp.exp2(oth_s[h] - top)
        shrink = jnp.exp2(near_top - top)
        total = notes[heads + h : heads + h + 1] * shrink + jnp.sum(
            e_other, axis=0, keepdims=True
        )
        delta = (
            notes[2 * heads + h : 2 * heads + h + 1] * shrink
            + jnp.sum(e_other * oth_dp[h], axis=0, keepdims=True)
        ) / total
        prob = jnp.exp2(own_s[h] - (top + jnp.log2(total)))
        own_low.append(prob.astype(bf16))
        own_ds.append((prob * (own_dp[h] - delta)).astype(bf16))
    for h, cut in enumerate(cuts):
        dk_ref[cut, :] = (dk_ref[cut, :] + mm(q_ft[cut], own_ds[h], NT)) * factor
        dv_ref[cut, :] += mm(g_ft[cut], own_low[h], NT)
    att_out[...] = flipped(att_ref[...])
    dq_out[...] = flipped(dq_ref[...])
    dk_out[...] = flipped(dk_ref[...])
    dv_out[...] = flipped(dv_ref[...])


def write_out(*refs):
    ends = refs[8]
    copies = [pltpu.make_async_copy(refs[i], refs[4 + i], ends.at[i]) for i in range(4)]
    for copy in copies:
        copy.start()
    for copy in copies:
        copy.wait()


def small_body(queries, key_rows, value_rows, grad_out, offsets):
    rows, width = queries.shape
    heads = width // HDIM
    seq_count = lax.axis_size("seq")
    hbm = pl.BlockSpec(memory_space=pltpu.HBM)
    vmem = pl.BlockSpec(memory_space=pltpu.VMEM)
    dma = pltpu.SemaphoreType.DMA
    outs = pl.pallas_call(
        functools.partial(kernel, seq_count, heads),
        out_shape=[jax.ShapeDtypeStruct((rows, width), jnp.bfloat16)] * 4,
        in_specs=[hbm] * 5,
        out_specs=[vmem] * 4,
        scratch_shapes=[
            pltpu.SMEM(offsets.shape, jnp.int32),
            *[pltpu.VMEM((rows, width), jnp.bfloat16)] * 4,
            *[pltpu.VMEM((width, rows), jnp.float32)] * 4,
            dma((5,)),
            pltpu.VMEM((8, 16, width), jnp.bfloat16),
            pltpu.VMEM((4, 16, width), jnp.bfloat16),
            pltpu.VMEM((8, SEG, 128), jnp.float32),
            pltpu.VMEM((heads, rows, rows), jnp.float32),
            pltpu.VMEM((heads, rows, rows), jnp.float32),
            pltpu.VMEM((heads, 8 * SEG, rows), jnp.float32),
            pltpu.VMEM((heads, 8 * SEG, 5 * SEG), jnp.float32),
            pltpu.VMEM((heads, rows, 5 * SEG), jnp.float32),
            dma((8,)), dma((8,)), dma((4,)), dma((4,)), dma((8,)), dma((8,)),
        ],
        compiler_params=pltpu.CompilerParams(
            collective_id=0, has_side_effects=True, vmem_limit_bytes=62 * 2**20
        ),
    )(offsets, queries, key_rows, value_rows, grad_out)
    return pl.pallas_call(
        write_out,
        out_shape=[jax.ShapeDtypeStruct((rows, width), jnp.bfloat16)] * 4,
        in_specs=[vmem] * 4,
        out_specs=[hbm] * 4,
        scratch_shapes=[dma((4,))],
    )(*outs)


def body(queries, key_rows, value_rows, grad_out, offsets):
    rows, width = queries.shape
    seq_count = lax.axis_size("seq")
    if seq_count == 8 and rows == 128 and width == 8 * HDIM:
        return small_body(queries, key_rows, value_rows, grad_out, offsets)
    return general_body(queries, key_rows, value_rows, grad_out, offsets)


def solution(mesh):
    placed = (
        P(("groups", "seq"), "head"),
        P(("groups", "seq"), "head"),
        P(("groups", "seq"), "head"),
        P(("groups", "seq"), "head"),
        P(),
    )
    return jax.shard_map(
        body,
        mesh=mesh,
        in_specs=placed,
        out_specs=(
            P(("groups", "seq"), "head"),
            P(("groups", "seq"), "head"),
            P(("groups", "seq"), "head"),
            P(("groups", "seq"), "head"),
        ),
        check_vma=False,
    )
```

```python
import functools
import math

import jax
import jax.numpy as jnp
from jax import lax
from jax.experimental import pallas as pl
from jax.experimental.pallas import tpu as pltpu
from jax.sharding import PartitionSpec as P

HDIM = 48
LEVELS = 8


def swapped(shard, axis, bit):
    return lax.ppermute(shard, axis, [(i, i ^ 1 << bit) for i in range(lax.axis_size(axis))])


def pick_rows(values, level_offsets, stride):
    if stride == 1:
        return values
    length, head_count = (values.shape[0], values.shape[1])
    trailing = values.shape[2:]
    grouped = values.reshape((length // stride, stride, head_count) + trailing)
    marks = jnp.arange(stride, dtype=jnp.int32)[:, None] == level_offsets[None, :]
    marks = marks.reshape((1, stride, head_count) + (1,) * len(trailing))
    kept = jnp.where(marks, grouped, jnp.zeros((), values.dtype))
    return jnp.sum(kept, axis=1, dtype=values.dtype)


def spread_rows(values, level_offsets, stride, fill):
    count, head_count = (values.shape[0], values.shape[1])
    trailing = values.shape[2:]
    marks = jnp.arange(stride, dtype=jnp.int32)[:, None] == level_offsets[None, :]
    marks = marks.reshape((1, stride, head_count) + (1,) * len(trailing))
    placed = jnp.where(marks, values[:, None], jnp.asarray(fill, values.dtype))
    return placed.reshape((count * stride, head_count) + trailing)


def pair_bits(count):
    return list(range(count))


def send_pairs(block_rows, bit_no):
    return swapped(block_rows, "seq", bit_no)


def send_partials(block_rows, bit_no):
    return swapped(block_rows.astype(jnp.bfloat16), "seq", bit_no).astype(block_rows.dtype)


def double_up(block_rows, bit_list, sender):
    position = lax.axis_index("seq")
    for bit_no in bit_list:
        partner_rows = sender(block_rows, bit_no)
        upper_half = position // 2**bit_no % 2 == 1
        block_rows = jnp.where(
            upper_half,
            jnp.concatenate([partner_rows, block_rows], 0),
            jnp.concatenate([block_rows, partner_rows], 0),
        )
    return block_rows


def halve_down(buffer, bit_list, sender):
    position = lax.axis_index("seq")
    for bit_no in reversed(bit_list):
        half_rows = buffer.shape[0] // 2
        lower_part, upper_part = (buffer[:half_rows], buffer[half_rows:])
        upper_half = position // 2**bit_no % 2 == 1
        kept_half = jnp.where(upper_half, upper_part, lower_part)
        given_half = jnp.where(upper_half, lower_part, upper_part)
        buffer = kept_half + sender(given_half, bit_no)
    return buffer


def head_blocks(heads_here):
    block_width = min(heads_here, 4)
    return [
        (first, min(first + block_width, heads_here)) for first in range(0, heads_here, block_width)
    ]


def forward_level(query_seg, key_seg, value_seg, factor):
    largest_list, total_list, summed_list = ([], [], [])
    for first, last in head_blocks(query_seg.shape[2]):
        scores = (
            jnp.einsum(
                "nihd,njhd->nhij",
                query_seg[:, :, first:last],
                key_seg[:, :, first:last],
                preferred_element_type=jnp.float32,
            )
            * factor
        )
        largest = jnp.max(scores, axis=3)
        powers = jnp.exp(scores - largest[..., None])
        largest_list.append(largest)
        total_list.append(jnp.sum(powers, axis=3))
        summed_list.append(
            jnp.einsum(
                "nhij,njhd->nihd",
                powers.astype(jnp.bfloat16),
                value_seg[:, :, first:last],
                preferred_element_type=jnp.float32,
            )
        )
    return (
        jnp.concatenate(largest_list, 1),
        jnp.concatenate(total_list, 1),
        jnp.concatenate(summed_list, 2),
    )


def level_grads(query_seg, key_seg, value_seg, outgrad_seg, total_seg, dot_seg, factor):
    query_list, key_list, value_list = ([], [], [])
    for first, last in head_blocks(query_seg.shape[2]):
        query_part = query_seg[:, :, first:last]
        key_block = key_seg[:, :, first:last]
        outgrad_part = outgrad_seg[:, :, first:last]
        scores = (
            jnp.einsum("nihd,njhd->nhij", query_part, key_block, preferred_element_type=jnp.float32)
            * factor
        )
        weights = jnp.exp(scores - total_seg[:, first:last, :, None])
        grad_prob = jnp.einsum(
            "nihd,njhd->nhij",
            outgrad_part,
            value_seg[:, :, first:last],
            preferred_element_type=jnp.float32,
        )
        grad_score = (weights * (grad_prob - dot_seg[:, first:last, :, None])).astype(jnp.bfloat16)
        query_list.append(
            jnp.einsum("nhij,njhd->nihd", grad_score, key_block, preferred_element_type=jnp.float32)
            * factor
        )
        key_list.append(
            jnp.einsum(
                "nhij,nihd->njhd", grad_score, query_part, preferred_element_type=jnp.float32
            )
            * factor
        )
        value_list.append(
            jnp.einsum(
                "nhij,nihd->njhd",
                weights.astype(jnp.bfloat16),
                outgrad_part,
                preferred_element_type=jnp.float32,
            )
        )
    query_grad = jnp.concatenate(query_list, 2)
    key_grad = jnp.concatenate(key_list, 2)
    value_grad = jnp.concatenate(value_list, 2)
    return (query_grad, key_grad, value_grad)


def general_body(queries, key_rows, value_rows, grad_out, offsets):
    row_count = queries.shape[0]
    width_here = queries.shape[1]
    heads_here = width_here // HDIM
    factor = HDIM ** (-0.5)
    seq_count = lax.axis_size("seq")
    segment = row_count * seq_count // 2 ** (LEVELS - 1)
    head_first = lax.axis_index("head") * heads_here
    offsets_here = lax.dynamic_slice_in_dim(offsets, head_first, heads_here, 1)
    query_all = queries.reshape(row_count, heads_here, HDIM)
    key_all = key_rows.reshape(row_count, heads_here, HDIM)
    value_all = value_rows.reshape(row_count, heads_here, HDIM)
    outgrad_all = grad_out.reshape(row_count, heads_here, HDIM)
    levels_kept = []
    for level_no in range(LEVELS):
        stride = 2**level_no
        seg_span = segment * stride
        picked = row_count // stride
        level_offsets = offsets_here[level_no]
        query_lev = pick_rows(query_all, level_offsets, stride)
        key_lev = pick_rows(key_all, level_offsets, stride)
        value_lev = pick_rows(value_all, level_offsets, stride)
        if seg_span <= row_count:
            pieces = row_count // seg_span
            bit_list = []
            query_seg = query_lev.reshape(pieces, segment, heads_here, HDIM)
            key_seg = key_lev.reshape(pieces, segment, heads_here, HDIM)
            value_seg = value_lev.reshape(pieces, segment, heads_here, HDIM)
        else:
            group_size = seg_span // row_count
            packed = jnp.concatenate(
                [key_lev.reshape(picked, width_here), value_lev.reshape(picked, width_here)], 1
            )
            if group_size == seq_count:
                bit_list = list(range(group_size.bit_length() - 1))
                gathered = lax.all_gather(packed, "seq", axis=0, tiled=True)
            else:
                bit_list = pair_bits(group_size.bit_length() - 1)
                gathered = double_up(packed, bit_list, send_pairs)
            query_seg = query_lev.reshape(1, picked, heads_here, HDIM)
            key_seg = gathered[:, :width_here].reshape(1, segment, heads_here, HDIM)
            value_seg = gathered[:, width_here:].reshape(1, segment, heads_here, HDIM)
        largest, totals, summed = forward_level(query_seg, key_seg, value_seg, factor)
        level_max = spread_rows(
            jnp.transpose(largest, (0, 2, 1)).reshape(picked, heads_here),
            level_offsets,
            stride,
            -jnp.inf,
        )
        level_total = spread_rows(
            jnp.transpose(totals, (0, 2, 1)).reshape(picked, heads_here), level_offsets, stride, 0.0
        )
        level_sum = spread_rows(
            summed.reshape(picked, heads_here, HDIM), level_offsets, stride, 0.0
        )
        if level_no == 0:
            running_max, running_total, running_sum = (level_max, level_total, level_sum)
        else:
            newest_max = jnp.maximum(running_max, level_max)
            old_scale = jnp.exp(running_max - newest_max)
            new_scale = jnp.exp(level_max - newest_max)
            running_total = running_total * old_scale + level_total * new_scale
            running_sum = running_sum * old_scale[..., None] + level_sum * new_scale[..., None]
            running_max = newest_max
        levels_kept.append(
            (
                stride,
                level_offsets,
                seg_span,
                bit_list,
                query_lev,
                key_lev,
                value_lev,
                query_seg,
                key_seg,
                value_seg,
            )
        )
    attended = (running_sum / running_total[..., None]).astype(jnp.bfloat16)
    log_total = running_max + jnp.log(running_total)
    dot_rows = jnp.sum(outgrad_all.astype(jnp.float32) * attended.astype(jnp.float32), axis=2)
    grad_q_sum = jnp.zeros((row_count, heads_here, HDIM), jnp.float32)
    grad_k_sum = jnp.zeros((row_count, heads_here, HDIM), jnp.float32)
    grad_v_sum = jnp.zeros((row_count, heads_here, HDIM), jnp.float32)
    for (
        stride,
        level_offsets,
        seg_span,
        bit_list,
        query_lev,
        key_lev,
        value_lev,
        query_seg,
        key_seg,
        value_seg,
    ) in levels_kept:
        picked = row_count // stride
        outgrad_lev = pick_rows(outgrad_all, level_offsets, stride)
        total_lev = pick_rows(log_total, level_offsets, stride)
        dot_lev = pick_rows(dot_rows, level_offsets, stride)
        pieces = query_seg.shape[0]
        rows_each = query_seg.shape[1]
        outgrad_seg = outgrad_lev.reshape(pieces, rows_each, heads_here, HDIM)
        total_seg = jnp.transpose(total_lev.reshape(pieces, rows_each, heads_here), (0, 2, 1))
        dot_seg = jnp.transpose(dot_lev.reshape(pieces, rows_each, heads_here), (0, 2, 1))
        if seg_span <= row_count:
            grad_query_lev, key_part, value_part = level_grads(
                query_seg, key_seg, value_seg, outgrad_seg, total_seg, dot_seg, factor
            )
            key_grad = key_part.reshape(picked, heads_here, HDIM)
            value_grad = value_part.reshape(picked, heads_here, HDIM)
        else:
            grad_query_lev, key_part, value_part = level_grads(
                query_seg, key_seg, value_seg, outgrad_seg, total_seg, dot_seg, factor
            )
            packed = jnp.concatenate(
                [key_part.reshape(segment, width_here), value_part.reshape(segment, width_here)], 1
            )
            own_rows = halve_down(packed, bit_list, send_partials)
            key_grad = own_rows[:, :width_here].reshape(picked, heads_here, HDIM)
            value_grad = own_rows[:, width_here:].reshape(picked, heads_here, HDIM)
        grad_q_sum = grad_q_sum + spread_rows(
            grad_query_lev.reshape(picked, heads_here, HDIM), level_offsets, stride, 0.0
        )
        grad_k_sum = grad_k_sum + spread_rows(key_grad, level_offsets, stride, 0.0)
        grad_v_sum = grad_v_sum + spread_rows(value_grad, level_offsets, stride, 0.0)
    return (
        attended.reshape(row_count, width_here),
        grad_q_sum.reshape(row_count, width_here).astype(jnp.bfloat16),
        grad_k_sum.reshape(row_count, width_here).astype(jnp.bfloat16),
        grad_v_sum.reshape(row_count, width_here).astype(jnp.bfloat16),
    )


SEG = 8
LOCAL = 5
NEG = -1e30
NN = (((1,), (0,)), ((), ()))
NT = (((1,), (1,)), ((), ()))


def mm(lhs, rhs, dims=NN):
    return lax.dot_general(lhs, rhs, dims, preferred_element_type=jnp.float32)


def flipped(block):
    return block.astype(jnp.bfloat16).T


def window(head_no):
    first = head_no * HDIM
    return first // 128 * 128, -(-(first + HDIM) // 128) * 128


def zero_extended(rows, head_no):
    low, high = window(head_no)
    first = head_no * HDIM
    parts = []
    if first > low:
        parts.append(jnp.zeros((first - low, rows.shape[1]), rows.dtype))
    parts.append(rows[first : first + HDIM])
    if high > first + HDIM:
        parts.append(jnp.zeros((high - first - HDIM, rows.shape[1]), rows.dtype))
    return parts[0] if len(parts) == 1 else jnp.concatenate(parts, 0)


def kernel(
    seq_count, heads, offs_hbm, q_hbm, k_hbm, v_hbm, g_hbm,
    att_out, dq_out, dk_out, dv_out,
    offs, q_ref, k_ref, v_ref, g_ref, att_ref, dq_ref, dk_ref, dv_ref, fetch,
    att_low, dq_low, dk_low, dv_low, left,
    buf_kv, buf_qg, stat, e_scr, dp_scr, far_bias, other_bias, own_bias,
    send_kv, recv_kv, send_qg, recv_qg, send_st, recv_st,
):
    me = lax.axis_index("seq")
    fetches = [
        pltpu.make_async_copy(here, there, fetch.at[i])
        for i, (here, there) in enumerate(
            ((offs_hbm, offs), (q_hbm, q_ref), (k_hbm, k_ref), (v_hbm, v_ref), (g_hbm, g_ref))
        )
    ]
    for copy in fetches:
        copy.start()
    leave = [
        pltpu.make_async_copy(here, there, left.at[i])
        for i, (here, there) in enumerate(
            ((att_low, att_out), (dq_low, dq_out), (dk_low, dk_out), (dv_low, dv_out))
        )
    ]
    f32, bf16 = jnp.float32, jnp.bfloat16
    factor = HDIM ** (-0.5)
    factor2 = factor * math.log2(math.e)
    rows = q_ref.shape[0]
    width = q_ref.shape[1]
    head_first = lax.axis_index("head") * heads

    def peer(dist):
        low = lax.rem(me, 2)
        mid = lax.rem(me // 2, 2)
        top = me // 4
        b0, b1, b2 = dist & 1, dist >> 1 & 1, dist >> 2
        low = 1 - low if b0 else low
        mid = 1 - mid if b1 else mid
        top = 1 - top if b2 else top
        return top * 4 + mid * 2 + low

    barrier = pltpu.get_barrier_semaphore()
    for dist in range(1, seq_count):
        pl.semaphore_signal(
            barrier, inc=1, device_id={"seq": peer(dist)}, device_id_type=pl.DeviceIdType.MESH
        )

    for copy in fetches:
        copy.wait()
    off = [[offs[lev, head_first + h] for h in range(heads)] for lev in range(LEVELS)]
    refs = (q_ref, k_ref, v_ref, g_ref)

    slot_no = lax.broadcasted_iota(jnp.int32, (SEG, rows), 0)
    lane_no = lax.broadcasted_iota(jnp.int32, (SEG, rows), 1)
    picks = []
    for h in range(heads):
        target = jnp.where(
            slot_no < 4,
            slot_no * 32 + off[5][h],
            jnp.where(slot_no < 6, (slot_no - 4) * 64 + off[6][h], off[7][h]),
        )
        target = jnp.where(slot_no == 7, -1, target)
        picks.append(target == lane_no)
    chosen = jnp.concatenate([jnp.where(p, 1.0, 0.0) for p in picks], 0).astype(bf16)
    col_head = lax.broadcasted_iota(jnp.int32, (SEG, width), 1)
    owns = []
    for a in range(4):
        got = mm(chosen, refs[a][...])
        own = jnp.zeros((SEG, width), f32)
        for h in range(heads):
            inside = (col_head >= h * HDIM) & (col_head < (h + 1) * HDIM)
            own = jnp.where(inside, got[h * SEG : (h + 1) * SEG], own)
        owns.append(own)
    q_own, k_own, v_own, g_own = owns
    last_row = lax.broadcasted_iota(jnp.int32, (SEG, width), 0) == SEG - 1
    k_own = jnp.where(last_row, q_own[6:7], k_own)
    v_own = jnp.where(last_row, g_own[6:7], v_own)
    buf_kv[0] = jnp.concatenate([k_own, v_own], 0).astype(bf16)
    buf_qg[0] = jnp.concatenate([q_own, g_own], 0).astype(bf16)

    pl.semaphore_wait(barrier, seq_count - 1)

    def remote(buf, send, recv, dist):
        return pltpu.make_async_remote_copy(
            src_ref=buf.at[0],
            dst_ref=buf.at[dist],
            send_sem=send.at[dist],
            recv_sem=recv.at[dist],
            device_id={"seq": peer(dist)},
            device_id_type=pl.DeviceIdType.MESH,
        )

    first = [remote(buf_kv, send_kv, recv_kv, d) for d in (7, 6, 5, 4, 3, 2, 1)]
    first += [remote(buf_qg, send_qg, recv_qg, d) for d in (3, 2, 1)]
    for copy in first:
        copy.start()

    qt, kt, vt, gt = [flipped(r[...]) for r in refs]

    feat_no = lax.broadcasted_iota(jnp.int32, (32, rows), 0)
    pos = lax.broadcasted_iota(jnp.int32, (32, rows), 1)
    feats = []
    starts = (0, 16, 24, 28, 30)
    place = feat_no - 0
    seg_of = pos // 8
    rest = pos & 0
    for lev in range(1, LOCAL):
        past = feat_no >= starts[lev]
        place = jnp.where(past, feat_no - starts[lev], place)
        seg_of = jnp.where(past, pos // (8 << lev), seg_of)
        rest = jnp.where(past, pos & ((1 << lev) - 1), rest)
    in_seg = (place == seg_of) & (feat_no < 31)
    for h in range(heads):
        wanted = jnp.where(feat_no >= 16, off[1][h], 0)
        for lev in range(2, LOCAL):
            wanted = jnp.where(feat_no >= starts[lev], off[lev][h], wanted)
        feats.append(jnp.where(in_seg & (rest == wanted), 1.0, 0.0))
    feat_rows = [
        jnp.concatenate(feats[4 * b : 4 * b + 4], 0).T.astype(bf16) for b in range(heads // 4)
    ]
    tops, sums, dots = [], [], []
    lane8 = lax.broadcasted_iota(jnp.int32, (SEG, 128), 1)
    row8 = lax.broadcasted_iota(jnp.int32, (SEG, 128), 0)
    note = jnp.where((row8 == SEG - 1) & (lane8 >= heads) & (lane8 < 2 * heads), 1.0, 0.0)
    scores, counts, dps = [], [], []
    for h in range(heads):
        low, high = window(h)
        before = 32 * (h % 4)
        parts = [jnp.zeros((before, rows), bf16)] if before else []
        parts.append(feats[h].astype(bf16))
        if before < 96:
            parts.append(jnp.zeros((96 - before, rows), bf16))
        counts.append(mm(feat_rows[h // 4], jnp.concatenate(parts, 0)))
        scores.append(mm(k_ref[:, low:high], zero_extended(qt, h)) * factor2)
        dps.append(mm(v_ref[:, low:high], zero_extended(gt, h)))
    for h in range(heads):
        score = jnp.where(counts[h] > 0, scores[h], NEG)
        top = jnp.max(score, axis=0, keepdims=True)
        near = counts[h] * jnp.exp2(score - top)
        e_scr[h] = near
        dp_scr[h] = dps[h]
        tops.append(top)
        sums.append(jnp.sum(near, axis=0, keepdims=True))
        dots.append(jnp.sum(near * dps[h], axis=0, keepdims=True))
    for h in range(heads):
        for kind, row in enumerate((tops[h], sums[h], dots[h])):
            column = jnp.sum(jnp.where(picks[h], row, 0.0), axis=1, keepdims=True)
            here = (lane8 == kind * heads + h) & (row8 < SEG - 1)
            note = jnp.where(here, column, note)
    stat[0] = note
    second = [remote(stat, send_st, recv_st, d) for d in (7, 6, 5, 4, 3, 2, 1)]
    for copy in second:
        copy.start()

    for h in range(heads):
        cut = slice(h * HDIM, (h + 1) * HDIM)
        att_ref[cut, :] = mm(vt[cut], e_scr[h].astype(bf16))

    far_n = SEG * seq_count
    query_n = 5 * SEG
    key_no = lax.broadcasted_iota(jnp.int32, (far_n, 128), 0)
    key_slot = key_no & 7
    key_dist = key_no >> 3
    lane_pos = lax.broadcasted_iota(jnp.int32, (far_n, 128), 1)
    key_span = jnp.where(key_slot < 4, 31, jnp.where(key_slot < 6, 63, 127))
    key_reach = jnp.where(key_slot < 4, 1, jnp.where(key_slot < 6, 2, 3))
    lane_rest = lane_pos & key_span
    lane_ok = (key_dist >> key_reach) == 0

    def query_marks(shape):
        number = lax.broadcasted_iota(jnp.int32, shape, 1)
        dist = jnp.where(number < 32, number >> 3, number - 32)
        slot = jnp.where(number < 32, number & 7, 6)
        return number, dist, slot

    _, dist_b, slot_b = query_marks((far_n, query_n))
    pair_ok = ((dist_b ^ key_dist[:, :query_n]) >> key_reach[:, :query_n]) == 0
    number_c, dist_c, slot_c = query_marks((rows, query_n))
    reach_c = jnp.where(slot_c < 4, 1, jnp.where(slot_c < 6, 2, 3))
    span_c = jnp.where(slot_c < 4, 31, jnp.where(slot_c < 6, 63, 127))
    own_pos = lax.broadcasted_iota(jnp.int32, (rows, query_n), 0)
    rest_c = own_pos & span_c
    ok_c = ((dist_c >> reach_c) == 0) & (slot_c != 7) & ((number_c < 32) | (dist_c >= 4))

    for h in range(heads):
        wanted = jnp.where(key_slot < 4, off[5][h], jnp.where(key_slot < 6, off[6][h], off[7][h]))
        wanted = jnp.where(key_slot == 7, -1, wanted)
        far_bias[h] = jnp.where(lane_ok & (lane_rest == wanted), 0.0, NEG)
        spot = jnp.where(
            slot_b < 4,
            slot_b * 32 + off[5][h],
            jnp.where(slot_b < 6, (slot_b - 4) * 64 + off[6][h], off[7][h]),
        )
        meets = pair_ok & ((spot & key_span[:, :query_n]) == wanted[:, :query_n])
        other_bias[h] = jnp.where(meets, 0.0, NEG)
        wanted_c = jnp.where(slot_c < 4, off[5][h], jnp.where(slot_c < 6, off[6][h], off[7][h]))
        own_bias[h] = jnp.where(ok_c & (rest_c == wanted_c), 0.0, NEG)

    for copy in first:
        copy.wait()
    kv = buf_kv[...].astype(f32)
    qg = buf_qg[...].astype(f32)
    k_far32 = kv[:, 0:SEG].reshape(far_n, width)
    v_far32 = kv[:, SEG:].reshape(far_n, width)
    q_far32 = jnp.concatenate(
        [qg[:, 0:SEG].reshape(4 * SEG, width)] + [kv[d, SEG - 1 : SEG] for d in range(8)], 0
    )
    g_far32 = jnp.concatenate(
        [qg[:, SEG:].reshape(4 * SEG, width)] + [kv[d, 2 * SEG - 1 : 2 * SEG] for d in range(8)], 0
    )
    k_far, v_far = k_far32.astype(bf16), v_far32.astype(bf16)
    k_ft, v_ft, q_ft, g_ft = [
        x.T.astype(bf16) for x in (k_far32, v_far32, q_far32, g_far32)
    ]
    cuts = [slice(h * HDIM, (h + 1) * HDIM) for h in range(heads)]
    far_s, far_dp, oth_s, oth_dp, own_s, own_dp = [], [], [], [], [], []
    for h in range(heads):
        low, high = window(h)
        qz, gz = zero_extended(qt, h), zero_extended(gt, h)
        qfz, gfz = zero_extended(q_ft, h), zero_extended(g_ft, h)
        far_s.append(mm(k_far[:, low:high], qz) * factor2 + far_bias[h])
        far_dp.append(mm(v_far[:, low:high], gz))
        oth_s.append(mm(k_far[:, low:high], qfz) * factor2 + other_bias[h])
        oth_dp.append(mm(v_far[:, low:high], gfz))
        own_s.append(mm(k_ref[:, low:high], qfz) * factor2 + own_bias[h])
        own_dp.append(mm(v_ref[:, low:high], gfz))
    near_low, near_ds, far_low, far_ds = [], [], [], []
    for h in range(heads):
        top = jnp.maximum(tops[h], jnp.max(far_s[h], axis=0, keepdims=True))
        e_far = jnp.exp2(far_s[h] - top)
        shrink = jnp.exp2(tops[h] - top)
        total = sums[h] * shrink + jnp.sum(e_far, axis=0, keepdims=True)
        inv = 1.0 / total
        delta = (dots[h] * shrink + jnp.sum(e_far * far_dp[h], axis=0, keepdims=True)) * inv
        scale = shrink * inv
        near = e_scr[h] * scale
        e_far = e_far * inv
        near_low.append(near.astype(bf16))
        far_low.append(e_far.astype(bf16))
        near_ds.append((near * (dp_scr[h] - delta)).astype(bf16))
        far_ds.append((e_far * (far_dp[h] - delta)).astype(bf16))
        att_ref[cuts[h], :] = att_ref[cuts[h], :] * scale
    for h, cut in enumerate(cuts):
        att_ref[cut, :] += mm(v_ft[cut], far_low[h])
        dq_ref[cut, :] = (mm(kt[cut], near_ds[h]) + mm(k_ft[cut], far_ds[h])) * factor
        dk_ref[cut, :] = mm(qt[cut], near_ds[h], NT)
        dv_ref[cut, :] = mm(gt[cut], near_low[h], NT)
    att_low[...] = flipped(att_ref[...])
    leave[0].start()
    dq_low[...] = flipped(dq_ref[...])
    leave[1].start()
    for copy in second:
        copy.wait()
    st = stat[...]
    notes = jnp.concatenate(
        [st[0:4].reshape(4 * SEG, 128)] + [st[d, 6:7] for d in range(8)], 0
    ).T
    own_low, own_ds = [], []
    for h in range(heads):
        near_top = notes[h : h + 1]
        top = jnp.maximum(near_top, jnp.max(oth_s[h], axis=0, keepdims=True))
        e_other = jnp.exp2(oth_s[h] - top)
        shrink = jnp.exp2(near_top - top)
        total = notes[heads + h : heads + h + 1] * shrink + jnp.sum(
            e_other, axis=0, keepdims=True
        )
        delta = (
            notes[2 * heads + h : 2 * heads + h + 1] * shrink
            + jnp.sum(e_other * oth_dp[h], axis=0, keepdims=True)
        ) / total
        prob = jnp.exp2(own_s[h] - (top + jnp.log2(total)))
        own_low.append(prob.astype(bf16))
        own_ds.append((prob * (own_dp[h] - delta)).astype(bf16))
    for h, cut in enumerate(cuts):
        dk_ref[cut, :] = (dk_ref[cut, :] + mm(q_ft[cut], own_ds[h], NT)) * factor
        dv_ref[cut, :] += mm(g_ft[cut], own_low[h], NT)
    dk_low[...] = flipped(dk_ref[...])
    leave[2].start()
    dv_low[...] = flipped(dv_ref[...])
    leave[3].start()
    for copy in leave:
        copy.wait()


def write_out(*refs):
    ends = refs[8]
    copies = [pltpu.make_async_copy(refs[i], refs[4 + i], ends.at[i]) for i in range(4)]
    for copy in copies:
        copy.start()
    for copy in copies:
        copy.wait()


def small_body(queries, key_rows, value_rows, grad_out, offsets):
    rows, width = queries.shape
    heads = width // HDIM
    seq_count = lax.axis_size("seq")
    hbm = pl.BlockSpec(memory_space=pltpu.HBM)
    dma = pltpu.SemaphoreType.DMA
    outs = pl.pallas_call(
        functools.partial(kernel, seq_count, heads),
        out_shape=[jax.ShapeDtypeStruct((rows, width), jnp.bfloat16)] * 4,
        in_specs=[hbm] * 5,
        out_specs=[hbm] * 4,
        scratch_shapes=[
            pltpu.SMEM(offsets.shape, jnp.int32),
            *[pltpu.VMEM((rows, width), jnp.bfloat16)] * 4,
            *[pltpu.VMEM((width, rows), jnp.float32)] * 4,
            dma((5,)),
            *[pltpu.VMEM((rows, width), jnp.bfloat16)] * 4,
            dma((4,)),
            pltpu.VMEM((8, 16, width), jnp.bfloat16),
            pltpu.VMEM((4, 16, width), jnp.bfloat16),
            pltpu.VMEM((8, SEG, 128), jnp.float32),
            pltpu.VMEM((heads, rows, rows), jnp.float32),
            pltpu.VMEM((heads, rows, rows), jnp.float32),
            pltpu.VMEM((heads, 8 * SEG, rows), jnp.float32),
            pltpu.VMEM((heads, 8 * SEG, 5 * SEG), jnp.float32),
            pltpu.VMEM((heads, rows, 5 * SEG), jnp.float32),
            dma((8,)), dma((8,)), dma((4,)), dma((4,)), dma((8,)), dma((8,)),
        ],
        compiler_params=pltpu.CompilerParams(
            collective_id=0, has_side_effects=True, vmem_limit_bytes=62 * 2**20
        ),
    )(offsets, queries, key_rows, value_rows, grad_out)
    return pl.pallas_call(
        write_out,
        out_shape=[jax.ShapeDtypeStruct((rows, width), jnp.bfloat16)] * 4,
        in_specs=[hbm] * 4,
        out_specs=[hbm] * 4,
        scratch_shapes=[dma((4,))],
    )(*outs)


def body(queries, key_rows, value_rows, grad_out, offsets):
    rows, width = queries.shape
    seq_count = lax.axis_size("seq")
    if seq_count == 8 and rows == 128 and width == 8 * HDIM:
        return small_body(queries, key_rows, value_rows, grad_out, offsets)
    return general_body(queries, key_rows, value_rows, grad_out, offsets)


def solution(mesh):
    placed = (
        P(("groups", "seq"), "head"),
        P(("groups", "seq"), "head"),
        P(("groups", "seq"), "head"),
        P(("groups", "seq"), "head"),
        P(),
    )
    return jax.shard_map(
        body,
        mesh=mesh,
        in_specs=placed,
        out_specs=(
            P(("groups", "seq"), "head"),
            P(("groups", "seq"), "head"),
            P(("groups", "seq"), "head"),
            P(("groups", "seq"), "head"),
        ),
        check_vma=False,
    )
```
